128 devices in a mesh: row: 8 (over x_hi, z), col: 16 (over y, x_lo, core).
Axes of the slice: x: 4 (x_hi: 2, x_lo: 2; x = x_hi * 2 + x_lo), y: 4, z: 4, core: 2. Of those that a mesh axis runs over, the one named last changes fastest.
Arguments:
- voxels: bfloat16 [32, 128, 256, 256], P(None, 'row', 'col'), may hold values from -6 to 6
- target: bfloat16 [32, 128, 256, 256], P(None, 'row', 'col'), may hold values from -6 to 6
- weight: bfloat16 [2, 32, 32, 64, 64, 32], P(None, None, None, 'row', 'col'), may hold values from -0.75 to 0.75
Outputs:
- grad_voxels: bfloat16 [32, 128, 256, 256], P(None, 'row', 'col')
- grad_weight: bfloat16 [2, 32, 32, 64, 64, 32], P(None, None, None, 'row', 'col')
The draws below stay inside these ranges and needn't reach their ends.
All inputs are finite; a program needn't handle non-finite values.
Results may differ from the reference program's by a relative error of at most 0.0011.
Values sent between devices are 32-bit elements; how exact they have to be, the bound alone decides.
No kernel may reach another device: no remote copies, remote signals or barrier semaphores. Data moves between devices by JAX's collectives and lax.ppermute only.
A program may use at most 192 MiB of HBM per device.

```python
import jax
import jax.numpy as jnp
from jax import lax

C = 32
X = 128
Y = 256
Z = 256
MX = 32
MY = 64
MZ = 64


def block_scale(own_key, dims, split, low, top_value):
    loudness = 1.0
    for position, blocks in split:
        heights = jax.random.uniform(jax.random.fold_in(jax.random.fold_in(own_key, 6), position), (blocks,), jnp.float32, low / len(split), top_value / len(split))
        loudness = loudness * jnp.repeat(jnp.exp(heights), dims[position] // blocks).reshape((-1,) + (1,) * (len(dims) - 1 - position))
    return loudness


def scatter_about(rng, extent, spread, bound, pieces=(), kind=jnp.bfloat16):
    result = jax.random.normal(rng, extent, jnp.float32) * spread
    if len(pieces) > 0:
        result = block_scale(rng, extent, pieces, -0.22, 0.18) * result
    return jnp.clip(result, min=-bound, max=bound).astype(kind)


def setup_inputs(seed: int = 0) -> dict:
    keys = jax.random.split(jax.random.key(seed), 4)
    return {
        "voxels": scatter_about(keys[0], (C, X, Y, Z), 1.0, 6.0, ((1, 8), (2, 16))),
        "target": scatter_about(keys[1], (C, X, Y, Z), 1.0, 6.0, ((1, 8), (2, 16))),
        "weight": scatter_about(keys[2], (2, C, C, MY, MZ, MX), (2 * C) ** -0.5, 0.75, ((3, 8), (4, 16))),
    }


def kept_index(number, length, offset):
    return ((jnp.arange(number) + offset) % length).astype(jnp.int32)


def spectrum(volume):
    full = jnp.fft.fftn(volume) * (X * Y * Z) ** -0.5
    x_index = kept_index(MX, X, -(MX // 2))
    y_index = kept_index(MY, Y, -(MY // 2))
    z_index = kept_index(MZ, Z, 0)
    kept = full[x_index][:, y_index][:, :, z_index]
    kept = jnp.transpose(kept, (1, 2, 0))
    return jnp.stack([jnp.real(kept), jnp.imag(kept)])


def synthesis(modes):
    x_index = kept_index(MX, X, -(MX // 2))
    y_index = kept_index(MY, Y, -(MY // 2))
    z_index = kept_index(MZ, Z, 0)
    complex_modes = jnp.transpose(modes[0] + 1j * modes[1], (2, 0, 1))
    full = jnp.zeros((X, Y, Z), complex_modes.dtype)
    full = full.at[x_index[:, None, None], y_index[None, :, None], z_index[None, None, :]].set(complex_modes)
    return jnp.real(jnp.fft.ifftn(full)) * (X * Y * Z)


def mix(weights, spectra):
    highest = lax.Precision.HIGHEST
    real_out = jnp.einsum("cojki,cjki->ojki", weights[0], spectra[0], precision=highest) - jnp.einsum("cojki,cjki->ojki", weights[1], spectra[1], precision=highest)
    imag_out = jnp.einsum("cojki,cjki->ojki", weights[0], spectra[1], precision=highest) + jnp.einsum("cojki,cjki->ojki", weights[1], spectra[0], precision=highest)
    return jnp.stack([real_out, imag_out])


def adjoint(weights, cotangent):
    highest = lax.Precision.HIGHEST
    real_back = jnp.einsum("cojki,ojki->cjki", weights[0], cotangent[0], precision=highest) + jnp.einsum("cojki,ojki->cjki", weights[1], cotangent[1], precision=highest)
    imag_back = jnp.einsum("cojki,ojki->cjki", weights[0], cotangent[1], precision=highest) - jnp.einsum("cojki,ojki->cjki", weights[1], cotangent[0], precision=highest)
    return jnp.stack([real_back, imag_back])


def reference(voxels, target, weight):
    weights = weight.astype(jnp.float32)
    spectra = jnp.transpose(lax.map(spectrum, voxels.astype(jnp.float32)), (1, 0, 2, 3, 4))
    mixed = mix(weights, spectra)
    output = lax.map(synthesis, jnp.transpose(mixed, (1, 0, 2, 3, 4))) * (MX * MY * MZ) ** -0.5
    residual = output - target.astype(jnp.float32)
    factor = ((X * Y * Z) / (MX * MY * MZ)) ** 0.5
    cotangent = factor * jnp.transpose(lax.map(spectrum, residual), (1, 0, 2, 3, 4))
    real_grad = spectra[0][:, None] * cotangent[0][None] + spectra[1][:, None] * cotangent[1][None]
    imag_grad = spectra[0][:, None] * cotangent[1][None] - spectra[1][:, None] * cotangent[0][None]
    grad_weight = jnp.stack([real_grad, imag_grad]).astype(jnp.bfloat16)
    back = adjoint(weights, cotangent)
    grad_voxels = (lax.map(synthesis, jnp.transpose(back, (1, 0, 2, 3, 4))) * (X * Y * Z) ** -0.5).astype(jnp.bfloat16)
    return grad_voxels, grad_weight
```

```python
import math

import jax
import jax.numpy as jnp
from jax import lax
from jax.sharding import PartitionSpec as P

X = 128
Y = 256
Z = 256
MX = 32
MY = 64
MZ = 64


HIGHEST_PRECISION = lax.Precision.HIGHEST


def phases(number, length, offset):
    frequency = lax.iota(jnp.int32, number) + offset
    position = lax.iota(jnp.int32, length)
    turns = frequency[:, None] * position[None, :] % length
    return 2.0 * math.pi / length * turns.astype(jnp.float32)


def complex_forward(number, length, offset):
    angle = phases(number, length, offset).T
    cos_table = jnp.cos(angle)
    sin_table = jnp.sin(angle)
    first_rows = jnp.stack([cos_table, -sin_table], 1)
    second_rows = jnp.stack([sin_table, cos_table], 1)
    return jnp.stack([first_rows, second_rows], 0) * length ** (-0.5)


def complex_inverse(number, length, offset):
    angle = phases(number, length, offset)
    cos_table = jnp.cos(angle)
    sin_table = jnp.sin(angle)
    first_rows = jnp.stack([cos_table, sin_table], 1)
    second_rows = jnp.stack([-sin_table, cos_table], 1)
    return jnp.stack([first_rows, second_rows], 0)


def real_forward(number, length):
    angle = phases(number, length, 0).T
    paired = jnp.stack([jnp.cos(angle), -jnp.sin(angle)], 2)
    return paired.reshape(length, 2 * number) * length ** (-0.5)


def real_inverse(number, length):
    angle = phases(number, length, 0)
    paired = jnp.stack([jnp.cos(angle), -jnp.sin(angle)], 1)
    return paired.reshape(2 * number, length)


def per_device(voxels, target, weight):
    ky_local = weight.shape[3]
    kz_local = weight.shape[4]
    z_forward = real_forward(MZ, Z)
    y_forward = complex_forward(MY, Y, -(MY // 2))
    x_forward = complex_forward(MX, X, -(MX // 2))
    x_inverse = complex_inverse(MX, X, -(MX // 2))
    y_inverse = complex_inverse(MY, Y, -(MY // 2))
    z_inverse = real_inverse(MZ, Z)

    def along_y(received):
        shaped = received.reshape(received.shape[:3] + (kz_local, 2))
        lines = jnp.einsum("cxykr,ryRj->cxkjR", shaped, y_forward, precision=HIGHEST_PRECISION)
        return lines.reshape(lines.shape[:3] + (2 * MY,))

    def along_x(received):
        shaped = received.reshape(received.shape[:3] + (ky_local, 2))
        return jnp.einsum("cxkjr,rxRi->Rcjki", shaped, x_forward, precision=HIGHEST_PRECISION)

    def analysis(volume):
        spectra_z = jnp.einsum("cxyz,zq->cxyq", volume, z_forward, precision=HIGHEST_PRECISION)
        middle = along_y(lax.all_to_all(spectra_z, "col", split_axis=3, concat_axis=2, tiled=True))
        return along_x(lax.all_to_all(middle, "row", split_axis=3, concat_axis=1, tiled=True))

    def back_y(received):
        shaped = received.reshape(received.shape[:3] + (MY, 2))
        lines = jnp.einsum("cxkjs,sjRy->cxykR", shaped, y_inverse, precision=HIGHEST_PRECISION)
        return lines.reshape(lines.shape[:3] + (2 * kz_local,))

    def back_z(received):
        return jnp.einsum("cxyq,qz->cxyz", received, z_inverse, precision=HIGHEST_PRECISION)

    def synthesis(spectra):
        lines_x = jnp.einsum("scjki,siRx->cxkjR", spectra, x_inverse, precision=HIGHEST_PRECISION)
        lines_x = lines_x.reshape(lines_x.shape[:3] + (2 * ky_local,))
        middle = back_y(lax.all_to_all(lines_x, "row", split_axis=1, concat_axis=3, tiled=True))
        return back_z(lax.all_to_all(middle, "col", split_axis=2, concat_axis=3, tiled=True))

    def hermitian_partner(modes):
        plane = modes[:, :, :, 0, :]
        rows = lax.axis_size("row")
        same = lax.ppermute(plane, "row", [(b, rows - 1 - b) for b in range(rows)])
        edge = lax.ppermute(plane[:, :, :1], "row", [(b, rows - b) for b in range(1, rows)])
        by_ky = jnp.concatenate([edge, same[:, :, :0:-1]], 2)
        by_kx = jnp.concatenate([jnp.zeros_like(by_ky[..., :1]), by_ky[..., :0:-1]], 3)
        return (by_kx * jnp.array([1.0, -1.0], jnp.float32)[:, None, None, None])[:, :, :, None, :]

    weights = weight.astype(jnp.float32)
    spectra = analysis(voxels.astype(jnp.float32))
    real_out = jnp.einsum(
        "cojki,cjki->ojki", weights[0], spectra[0], precision=HIGHEST_PRECISION
    ) - jnp.einsum("cojki,cjki->ojki", weights[1], spectra[1], precision=HIGHEST_PRECISION)
    imag_out = jnp.einsum(
        "cojki,cjki->ojki", weights[0], spectra[1], precision=HIGHEST_PRECISION
    ) + jnp.einsum("cojki,cjki->ojki", weights[1], spectra[0], precision=HIGHEST_PRECISION)
    mixed = jnp.stack([real_out, imag_out])
    scale = 0.5 * math.sqrt(X * Y * Z / (MX * MY * MZ))
    factor = math.sqrt(X * Y * Z / (MX * MY * MZ))
    mirrored = hermitian_partner(mixed)
    first_plane = (lax.axis_index("col") == 0) & (jnp.arange(kz_local) == 0)
    output_spectra = scale * (mixed + jnp.where(first_plane[:, None], mirrored, 0.0))
    cotangent = factor * (output_spectra - analysis(target.astype(jnp.float32)))
    real_grad = spectra[0][:, None] * cotangent[0][None] + spectra[1][:, None] * cotangent[1][None]
    imag_grad = spectra[0][:, None] * cotangent[1][None] - spectra[1][:, None] * cotangent[0][None]
    grad_weight = jnp.stack([real_grad, imag_grad]).astype(jnp.bfloat16)
    real_back = jnp.einsum(
        "cojki,ojki->cjki", weights[0], cotangent[0], precision=HIGHEST_PRECISION
    ) + jnp.einsum("cojki,ojki->cjki", weights[1], cotangent[1], precision=HIGHEST_PRECISION)
    imag_back = jnp.einsum(
        "cojki,ojki->cjki", weights[0], cotangent[1], precision=HIGHEST_PRECISION
    ) - jnp.einsum("cojki,ojki->cjki", weights[1], cotangent[0], precision=HIGHEST_PRECISION)
    back = jnp.stack([real_back, imag_back])
    grad_voxels = (synthesis(back) * (X * Y * Z) ** (-0.5)).astype(jnp.bfloat16)
    return (grad_voxels, grad_weight)


def solution(mesh):
    placed = (
        P(None, "row", "col", None),
        P(None, "row", "col", None),
        P(None, None, None, "row", "col", None),
    )
    return jax.shard_map(
        per_device,
        mesh=mesh,
        in_specs=placed,
        out_specs=(P(None, "row", "col", None), P(None, None, None, "row", "col", None)),
        check_vma=False,
    )
```

```python
import functools
import math

import jax
import jax.numpy as jnp
import ml_dtypes
import numpy as np
from jax import lax
from jax.experimental import pallas as pl
from jax.experimental.pallas import tpu as pltpu
from jax.sharding import Mesh
from jax.sharding import PartitionSpec as P

C = 32
X = 128
Y = 256
Z = 256
MX = 32
MY = 64
MZ = 64

AXES = ("xh", "z", "y", "xl", "core")
SHAPE = (2, 4, 4, 2, 2)
ROW = ("xh", "z")
COL = ("y", "xl", "core")
FIRST = ("y", "core")
SECOND = ("xh", "z", "xl")
F32 = jnp.float32
BF16 = jnp.bfloat16


def split_parts(table):
    high = table.astype(ml_dtypes.bfloat16)
    low = (table - high.astype(np.float64)).astype(ml_dtypes.bfloat16)
    return high, low


def angles(frequency, position, length):
    return 2.0 * np.pi / length * ((frequency[:, None] * position[None, :]) % length)


def kept_z():
    y, core, part, xl, k = np.meshgrid(
        np.arange(4), np.arange(2), np.arange(2), np.arange(2), np.arange(4), indexing="ij"
    )
    return (((y * 2 + xl) * 2 + core) * 4 + k).reshape(-1), part.reshape(-1)


def z_table():
    frequency, part = kept_z()
    angle = angles(frequency, np.arange(Z), Z)
    return np.where(part[:, None] == 0, np.cos(angle), -np.sin(angle)) * Z**-0.5


def rotation(angle, row_part, column_part, sign):
    same = row_part[:, None] == column_part[None, :]
    lower = row_part[:, None] > column_part[None, :]
    return np.where(same, np.cos(angle), np.where(lower, sign, -sign) * np.sin(angle))


def y_points(xl):
    y, core, point, part = np.meshgrid(
        np.arange(4), np.arange(2), np.arange(16), np.arange(2), indexing="ij"
    )
    return (((y * 2 + xl) * 2 + core) * 16 + point).reshape(-1), part.reshape(-1)


def y_modes():
    block, part, j = np.meshgrid(np.arange(8), np.arange(2), np.arange(8), indexing="ij")
    return (block * 8 + j).reshape(-1) - MY // 2, part.reshape(-1)


def y_forward(xl):
    position, column_part = y_points(xl)
    frequency, row_part = y_modes()
    return rotation(angles(frequency, position, Y), row_part, column_part, -1) * Y**-0.5


def y_inverse(xl):
    position, row_part = y_points(xl)
    frequency, column_part = y_modes()
    return rotation(angles(frequency, position, Y).T, row_part, column_part, 1) * Y**-0.5


def x_points():
    return np.repeat(np.arange(X), 2), np.tile(np.arange(2), X)


def x_modes():
    return np.tile(np.arange(MX), 2) - MX // 2, np.repeat(np.arange(2), MX)


def x_forward():
    position, column_part = x_points()
    frequency, row_part = x_modes()
    return rotation(angles(frequency, position, X), row_part, column_part, -1) * X**-0.5


def x_inverse():
    position, row_part = x_points()
    frequency, column_part = x_modes()
    return rotation(angles(frequency, position, X).T, row_part, column_part, 1) * X**-0.5


def stacked(table):
    return np.concatenate(split_parts(table), 0)


def swap_table():
    index = np.arange(256)
    table = np.zeros((256, 256), ml_dtypes.bfloat16)
    table[index, (index % 16) * 16 + index // 16] = 1
    return table


def dot(a, b):
    return jnp.dot(a, b, preferred_element_type=F32)


def halves(values):
    high = values.astype(BF16)
    return high, (values - high.astype(F32)).astype(BF16)


def table_dot(table, values):
    rows = table.shape[0] // 2
    high, low = halves(values)
    both = dot(table, high)
    return both[:rows] + both[rows:] + dot(table[:rows], low)


def swap_quads(tiles):
    lane = lax.broadcasted_iota(jnp.int32, tiles[0].shape, 1) // 32
    result = []
    for b in range(4):
        total = None
        for a in range(4):
            shift = (32 * (a - b)) % 128
            moved = pltpu.roll(tiles[a], shift, 1) if shift else tiles[a]
            total = moved if total is None else jnp.where(lane == a, moved, total)
        result.append(total)
    return result


def z_forward_kernel(volume, swap, table, out, rows):
    for x in range(4):
        for half in range(2):
            block = volume[half * 16 : half * 16 + 16, x].reshape(256, Z)
            moved = dot(swap[...], block).astype(BF16)
            for y in range(16):
                rows[y, x, half * 16 : half * 16 + 16, :] = moved[y * 16 : y * 16 + 16]
    for pair in range(8):
        points = rows[pair * 2 : pair * 2 + 2].reshape(256, Z)
        both = lax.dot_general(
            table[...], points, (((1,), (1,)), ((), ())), preferred_element_type=F32
        )
        values = both[:128] + both[128:]
        for y in range(2):
            for target in range(8):
                for part in range(2):
                    row = (target * 2 + part) * 8
                    out[target, 0, pair * 2 + y, part] = values[row : row + 8, y * 128 : y * 128 + 128]


def y_forward_kernel(received, table, out):
    for quad in range(2):
        columns = []
        for k in range(4):
            kz = quad * 4 + k
            columns.append(
                jnp.concatenate(
                    [received[s, 0, pl.ds(kz, 32, stride=8), :] for s in range(8)], 0
                )
            )
        values = table_dot(table[...], jnp.concatenate(columns, 1))
        tiles = swap_quads([values[:, k * 128 : k * 128 + 128] for k in range(4)])
        for x in range(4):
            for block in range(8):
                for part in range(2):
                    row = (block * 2 + part) * 8
                    out[block * 2 + quad, x, part] = tiles[x][row : row + 8]


def x_forward_kernel(received, table, out, flat):
    for ky in range(8):
        pieces = []
        for block in range(8):
            first = received[block * 2, pl.ds(ky, 32, stride=8), :]
            second = received[block * 2 + 1, pl.ds(ky, 32, stride=8), :]
            pieces.append(first + second)
        values = table_dot(table[...], jnp.concatenate(pieces, 0))
        for part in range(2):
            flat[2 + part, ky * 32 : ky * 32 + 32] = values[part * 32 : part * 32 + 32]
    for part in range(2):
        for high in range(2):
            block = flat[2 + part, high * 128 : high * 128 + 128]
            flat[part, high * 128 : high * 128 + 128] = block.T
        for c in range(C):
            out[part, c] = flat[part, pl.ds(c, 8, stride=32), :]


def mix_kernel(weight, spectra, out):
    for o in range(0, 8, 4):
        rows = slice(o * 8, o * 8 + 32)

        def step(c, totals):
            real, imag = totals
            weight_real = weight[0, c, rows].astype(F32)
            weight_imag = weight[1, c, rows].astype(F32)
            field_real = jnp.concatenate([spectra[0, c]] * 4, 0)
            field_imag = jnp.concatenate([spectra[1, c]] * 4, 0)
            real = real + weight_real * field_real - weight_imag * field_imag
            imag = imag + weight_real * field_imag + weight_imag * field_real
            return real, imag

        zero = jnp.zeros((32, 128), F32)
        real, imag = lax.fori_loop(0, C, step, (zero, zero), unroll=4)
        out[0, rows] = real
        out[1, rows] = imag


def back_kernel(weight, mixed, partner, target, back, cotangent):
    factor = math.sqrt(X * Y * Z / (MX * MY * MZ))

    @pl.when(pl.program_id(0) == 0)
    def _():
        cotangent[...] = (0.5 * factor * factor) * (mixed[...] + partner[...]) - factor * target[...]

    def step(c, carry):
        real = jnp.zeros((32, 128), F32)
        imag = jnp.zeros((32, 128), F32)
        for o in range(0, C, 4):
            rows = slice(o * 8, o * 8 + 32)
            weight_real = weight[0, c, rows].astype(F32)
            weight_imag = weight[1, c, rows].astype(F32)
            real = real + weight_real * cotangent[0, rows] + weight_imag * cotangent[1, rows]
            imag = imag + weight_real * cotangent[1, rows] - weight_imag * cotangent[0, rows]
        back[0, c] = real[:8] + real[8:16] + real[16:24] + real[24:]
        back[1, c] = imag[:8] + imag[8:16] + imag[16:24] + imag[24:]
        return carry

    lax.fori_loop(0, 8, step, 0)


def weight_grad_kernel(spectra, cotangent, out):
    def step(c, carry):
        field_real = jnp.concatenate([spectra[0, c]] * 4, 0)
        field_imag = jnp.concatenate([spectra[1, c]] * 4, 0)
        for o in range(0, C, 4):
            rows = slice(o * 8, o * 8 + 32)
            real, imag = cotangent[0, rows], cotangent[1, rows]
            out[0, c, rows] = (field_real * real + field_imag * imag).astype(BF16)
            out[1, c, rows] = (field_real * imag - field_imag * real).astype(BF16)
        return carry

    lax.fori_loop(0, 8, step, 0)


def x_inverse_kernel(back, table, out, flat):
    for part in range(2):
        for c in range(C):
            flat[part, pl.ds(c, 8, stride=32), :] = back[part, c]
    for high in range(2):
        turned = [flat[part, high * 128 : high * 128 + 128].T for part in range(2)]
        for low in range(4):
            ky = high * 4 + low
            modes = jnp.concatenate([t[low * 32 : low * 32 + 32] for t in turned], 0)
            values = table_dot(table[...], modes)
            for block in range(8):
                for xl in range(2):
                    out[block * 2 + xl, pl.ds(ky, 32, stride=8), :] = values[
                        block * 32 : block * 32 + 32
                    ]


def y_inverse_kernel(received, table, out):
    for quad in range(2):
        tiles = []
        for x in range(4):
            tiles.append(
                jnp.concatenate(
                    [received[block * 2 + quad, x].reshape(16, 128) for block in range(8)], 0
                )
            )
        columns = swap_quads(tiles)
        values = table_dot(table[...], jnp.concatenate(columns, 1))
        for k in range(4):
            for target in range(8):
                out[target, 0, pl.ds(quad * 4 + k, 32, stride=8), :] = values[
                    target * 32 : target * 32 + 32, k * 128 : k * 128 + 128
                ]


def z_inverse_kernel(received, swap, table, out, rows):
    for y in range(16):
        modes = jnp.concatenate([received[s, 0, y].reshape(16, 128) for s in range(8)], 0)
        high, low = halves(modes.T)
        both = jnp.concatenate([high, low], 1)
        first = jnp.concatenate([table[:128], table[:128]], 0)
        values = dot(both, first) + dot(high, table[128:])
        rows[y] = values.astype(BF16).reshape(4, 32, Z)
    for x in range(4):
        for half in range(2):
            block = jnp.concatenate(
                [rows[y, x, half * 16 : half * 16 + 16, :] for y in range(16)], 0
            )
            moved = dot(swap[...], block).astype(BF16)
            out[half * 16 : half * 16 + 16, x] = moved.reshape(16, 16, Z)


def call(kernel, out, grid, in_specs, out_specs, scratch=(), cost=None):
    return pl.pallas_call(
        kernel,
        out_shape=out,
        grid=grid,
        in_specs=in_specs,
        out_specs=out_specs,
        scratch_shapes=list(scratch),
        compiler_params=pltpu.CompilerParams(vmem_limit_bytes=40 * 2**20),
        cost_estimate=cost,
    )


def whole(*dims):
    return pl.BlockSpec(dims, lambda *i: (0,) * len(dims))


def struct(*dims, kind=F32):
    return jax.ShapeDtypeStruct(dims, kind)


def estimate(flops, moved):
    return pl.CostEstimate(flops=flops, bytes_accessed=moved, transcendentals=0)


def z_forward_call(volume):
    return call(
        z_forward_kernel,
        struct(8, 4, 16, 2, 8, 128),
        (4,),
        [
            pl.BlockSpec((32, 4, 16, Z), lambda i: (0, i, 0, 0)),
            whole(256, 256),
            whole(256, Z),
        ],
        pl.BlockSpec((8, 1, 16, 2, 8, 128), lambda i: (0, i, 0, 0, 0, 0)),
        [pltpu.VMEM((16, 4, 32, Z), BF16)],
        estimate(3 * 2**30, 8 * 2**20),
    )(volume, jnp.asarray(swap_table()), jnp.asarray(stacked(z_table())))


def y_forward_call(received, table):
    return call(
        y_forward_kernel,
        struct(16, 16, 2, 8, 128),
        (4,),
        [
            pl.BlockSpec((8, 1, 256, 128), lambda i: (0, i, 0, 0)),
            whole(256, 256),
        ],
        pl.BlockSpec((16, 4, 2, 8, 128), lambda i: (0, i, 0, 0, 0)),
        (),
        estimate(2 * 2**30, 6 * 2**20),
    )(received.reshape(8, 4, 256, 128), table)


def x_forward_call(received):
    return call(
        x_forward_kernel,
        struct(2, 32, 8, 128),
        (),
        [whole(16, 256, 128), whole(128, 256)],
        whole(2, 32, 8, 128),
        [pltpu.VMEM((4, 256, 128), F32)],
        estimate(2**28, 3 * 2**20),
    )(received.reshape(16, 256, 128), jnp.asarray(stacked(x_forward())))


def mix_call(weight, spectra):
    return call(
        mix_kernel,
        struct(2, 256, 128),
        (4,),
        [
            pl.BlockSpec((2, 32, 64, 128), lambda i: (0, 0, i, 0)),
            whole(2, 32, 8, 128),
        ],
        pl.BlockSpec((2, 64, 128), lambda i: (0, i, 0)),
        (),
        estimate(2**27, 5 * 2**20),
    )(weight, spectra)


def back_call(weight, mixed, partner, target):
    small = whole(2, 256, 128)
    return call(
        back_kernel,
        (struct(2, 32, 8, 128), struct(2, 256, 128)),
        (4,),
        [pl.BlockSpec((2, 8, 256, 128), lambda i: (0, i, 0, 0)), small, small, small],
        (pl.BlockSpec((2, 8, 8, 128), lambda i: (0, i, 0, 0)), small),
        (),
        estimate(2**27, 5 * 2**20),
    )(weight, mixed, partner, target)


def weight_grad_call(spectra, cotangent):
    return call(
        weight_grad_kernel,
        struct(2, 32, 256, 128, kind=BF16),
        (4,),
        [pl.BlockSpec((2, 8, 8, 128), lambda i: (0, i, 0, 0)), whole(2, 256, 128)],
        pl.BlockSpec((2, 8, 256, 128), lambda i: (0, i, 0, 0)),
        (),
        estimate(2**27, 5 * 2**20),
    )(spectra, cotangent)


def x_inverse_call(back):
    return call(
        x_inverse_kernel,
        struct(16, 256, 128),
        (),
        [whole(2, 32, 8, 128), whole(512, 64)],
        whole(16, 256, 128),
        [pltpu.VMEM((2, 256, 128), F32)],
        estimate(2**28, 3 * 2**20),
    )(back, jnp.asarray(stacked(x_inverse())))


def y_inverse_call(received, table):
    return call(
        y_inverse_kernel,
        struct(8, 4, 256, 128),
        (4,),
        [
            pl.BlockSpec((16, 4, 2, 8, 128), lambda i: (0, i, 0, 0, 0)),
            whole(512, 128),
        ],
        pl.BlockSpec((8, 1, 256, 128), lambda i: (0, i, 0, 0)),
        (),
        estimate(2 * 2**30, 6 * 2**20),
    )(received.reshape(16, 16, 2, 8, 128), table)


def z_inverse_call(received):
    return call(
        z_inverse_kernel,
        struct(32, 16, 16, Z, kind=BF16),
        (4,),
        [
            pl.BlockSpec((8, 1, 16, 2, 8, 128), lambda i: (0, i, 0, 0, 0, 0)),
            whole(256, 256),
            whole(256, Z),
        ],
        pl.BlockSpec((32, 4, 16, Z), lambda i: (0, i, 0, 0)),
        [pltpu.VMEM((16, 4, 32, Z), BF16)],
        estimate(3 * 2**30, 8 * 2**20),
    )(
        received.reshape(8, 4, 16, 2, 8, 128),
        jnp.asarray(swap_table()),
        jnp.asarray(stacked(z_table())),
    )


def exchange(values, axes):
    return lax.all_to_all(values, axes, split_axis=0, concat_axis=0, tiled=True)


def plane_pairs():
    index = np.arange(math.prod(SHAPE)).reshape(8, 16)[:, 0].tolist()
    same = [(index[b], index[7 - b]) for b in range(8)]
    edge = [(index[b], index[8 - b]) for b in range(1, 8)]
    return same, edge


def mirrored(mixed):
    same_pairs, edge_pairs = plane_pairs()
    plane = mixed.reshape(2, C, 2, 4, 4, MX)[:, :, :, 0].reshape(2, C, 8, MX)
    same = lax.ppermute(plane, AXES, same_pairs)
    edge = lax.ppermute(plane[:, :, :1], AXES, edge_pairs)
    by_ky = jnp.concatenate([edge, same[:, :, :0:-1]], 2)
    by_kx = jnp.concatenate([jnp.zeros_like(by_ky[..., :1]), by_ky[..., :0:-1]], 3)
    signed = by_kx * jnp.array([1.0, -1.0], F32)[:, None, None, None]
    padded = jnp.pad(signed.reshape(2, C, 2, 1, 4, MX), ((0, 0),) * 3 + ((0, 3),) + ((0, 0),) * 2)
    return padded.reshape(2, 256, 128)


def per_device(voxels, target, weight):
    xl = lax.axis_index("xl")
    forward = jnp.asarray(np.stack([stacked(y_forward(0)), stacked(y_forward(1))]))[xl]
    inverse = jnp.asarray(np.stack([stacked(y_inverse(0)), stacked(y_inverse(1))]))[xl]

    def analysis(volume):
        lines = exchange(z_forward_call(volume), FIRST)
        planes = exchange(y_forward_call(lines, forward), SECOND)
        return x_forward_call(planes)

    packed = weight.reshape(2, C, C, 2, 4, 4, MX).transpose(0, 1, 2, 3, 5, 4, 6)
    packed = packed.reshape(2, C, 256, 128)
    spectra = analysis(voxels)
    target_spectra = analysis(target)
    mixed = mix_call(packed, spectra)
    back, cotangent = back_call(
        packed, mixed, mirrored(mixed), target_spectra.reshape(2, 256, 128)
    )
    planes = exchange(x_inverse_call(back), SECOND)
    lines = exchange(y_inverse_call(planes, inverse), FIRST)
    grad_voxels = z_inverse_call(lines)
    grad = weight_grad_call(spectra, cotangent)
    grad = grad.reshape(2, C, C, 2, 4, 4, MX).transpose(0, 1, 2, 3, 5, 4, 6)
    return grad_voxels, grad.reshape(2, C, C, 8, 4, MX)


def solution(mesh):
    fine = Mesh(mesh.devices.reshape(SHAPE), AXES)
    field = P(None, ROW, COL, None)
    modes = P(None, None, None, ROW, COL, None)
    return jax.shard_map(
        per_device,
        mesh=fine,
        in_specs=(field, field, modes),
        out_specs=(field, modes),
        check_vma=False,
    )
```

```python
import functools
import math

import jax
import jax.numpy as jnp
import ml_dtypes
import numpy as np
from jax import lax
from jax.experimental import pallas as pl
from jax.experimental.pallas import tpu as pltpu
from jax.sharding import Mesh
from jax.sharding import PartitionSpec as P

C = 32
X = 128
Y = 256
Z = 256
MX = 32
MY = 64
MZ = 64

AXES = ("xh", "z", "y", "xl", "core")
SHAPE = (2, 4, 4, 2, 2)
ROW = ("xh", "z")
COL = ("y", "xl", "core")
FIRST = ("y", "core")
SECOND = ("xh", "z", "xl")
F32 = jnp.float32
BF16 = jnp.bfloat16


def split_parts(table):
    high = table.astype(ml_dtypes.bfloat16)
    low = (table - high.astype(np.float64)).astype(ml_dtypes.bfloat16)
    return high, low


def angles(frequency, position, length):
    return 2.0 * np.pi / length * ((frequency[:, None] * position[None, :]) % length)


def kept_z():
    y, core, part, xl, k = np.meshgrid(
        np.arange(4), np.arange(2), np.arange(2), np.arange(2), np.arange(4), indexing="ij"
    )
    return (((y * 2 + xl) * 2 + core) * 4 + k).reshape(-1), part.reshape(-1)


def z_table():
    frequency, part = kept_z()
    angle = angles(frequency, np.arange(Z), Z)
    return np.where(part[:, None] == 0, np.cos(angle), -np.sin(angle)) * Z**-0.5


def rotation(angle, row_part, column_part, sign):
    same = row_part[:, None] == column_part[None, :]
    lower = row_part[:, None] > column_part[None, :]
    return np.where(same, np.cos(angle), np.where(lower, sign, -sign) * np.sin(angle))


def y_points(xl):
    y, core, point, part = np.meshgrid(
        np.arange(4), np.arange(2), np.arange(16), np.arange(2), indexing="ij"
    )
    return (((y * 2 + xl) * 2 + core) * 16 + point).reshape(-1), part.reshape(-1)


def z_table_rows(order):
    half, part, place, k = np.meshgrid(
        np.arange(2), np.arange(2), np.arange(8), np.arange(4), indexing="ij"
    )
    frequency = np.array(order)[half * 8 + place] * 4 + k
    angle = angles(frequency.reshape(-1), np.arange(Z), Z)
    return np.where(part.reshape(-1, 1) == 0, np.cos(angle), -np.sin(angle)) * Z**-0.5


def y_forward_rows(places):
    block, part, point = np.meshgrid(
        np.array(places), np.arange(2), np.arange(16), indexing="ij"
    )
    frequency, row_part = y_modes()
    angle = angles(frequency, (block * 16 + point).reshape(-1), Y)
    return rotation(angle, row_part, part.reshape(-1), -1) * Y**-0.5


def y_modes():
    block, part, j = np.meshgrid(np.arange(8), np.arange(2), np.arange(8), indexing="ij")
    return (block * 8 + j).reshape(-1) - MY // 2, part.reshape(-1)


def y_forward(xl):
    position, column_part = y_points(xl)
    frequency, row_part = y_modes()
    return rotation(angles(frequency, position, Y), row_part, column_part, -1) * Y**-0.5


def y_inverse(xl):
    position, row_part = y_points(xl)
    frequency, column_part = y_modes()
    return rotation(angles(frequency, position, Y).T, row_part, column_part, 1) * Y**-0.5


def x_points():
    return np.repeat(np.arange(X), 2), np.tile(np.arange(2), X)


def x_modes():
    return np.tile(np.arange(MX), 2) - MX // 2, np.repeat(np.arange(2), MX)


def x_forward():
    position, column_part = x_points()
    frequency, row_part = x_modes()
    return rotation(angles(frequency, position, X), row_part, column_part, -1) * X**-0.5


def x_inverse():
    position, row_part = x_points()
    frequency, column_part = x_modes()
    return rotation(angles(frequency, position, X).T, row_part, column_part, 1) * X**-0.5


def stacked(table):
    return np.concatenate(split_parts(table), 0)


def swap_table():
    index = np.arange(256)
    table = np.zeros((256, 256), ml_dtypes.bfloat16)
    table[index, (index % 16) * 16 + index // 16] = 1
    return table


def dot(a, b):
    return jnp.dot(a, b, preferred_element_type=F32)


def halves(values):
    high = values.astype(BF16)
    return high, (values - high.astype(F32)).astype(BF16)


def table_dot(table, values):
    rows = table.shape[0] // 2
    high, low = halves(values)
    both = dot(table, high)
    return both[:rows] + both[rows:] + dot(table[:rows], low)


def swap_quads(tiles):
    lane = lax.broadcasted_iota(jnp.int32, tiles[0].shape, 1) // 32
    result = []
    for b in range(4):
        total = None
        for a in range(4):
            shift = (32 * (a - b)) % 128
            moved = pltpu.roll(tiles[a], shift, 1) if shift else tiles[a]
            total = moved if total is None else jnp.where(lane == a, moved, total)
        result.append(total)
    return result


def by_source(refs):
    crossed = refs[4]
    return [crossed.at[i, 0] if j else refs[i].at[0, 0] for i in range(4) for j in range(2)]


def z_forward_kernel(volume, swap, table, *refs):
    out, rows = refs[:4], refs[4]
    for x in range(4):
        for half in range(2):
            block = volume[half * 16 : half * 16 + 16, x].reshape(256, Z)
            moved = dot(swap[...], block).astype(BF16)
            for y in range(16):
                rows[y, x, half * 16 : half * 16 + 16, :] = moved[y * 16 : y * 16 + 16]
    for pair in range(8):
        points = rows[pair * 2 : pair * 2 + 2].reshape(256, Z)
        both = lax.dot_general(
            table[...], points, (((1,), (1,)), ((), ())), preferred_element_type=F32
        )
        values = both[:128] + both[128:]
        for y in range(2):
            for target in range(8):
                for part in range(2):
                    row = (target * 2 + part) * 8
                    out[target // 2][target % 2, 0, pair * 2 + y, part] = values[
                        row : row + 8, y * 128 : y * 128 + 128
                    ]


def y_forward_kernel(*refs):
    received, table, out = by_source(refs[:5]), refs[5], refs[6]
    for quad in range(2):
        columns = []
        for k in range(4):
            kz = quad * 4 + k
            columns.append(
                jnp.concatenate(
                    [received[s][pl.ds(kz, 32, stride=8), :] for s in range(8)], 0
                )
            )
        values = table_dot(table[...], jnp.concatenate(columns, 1))
        tiles = swap_quads([values[:, k * 128 : k * 128 + 128] for k in range(4)])
        for x in range(4):
            for block in range(8):
                for part in range(2):
                    row = (block * 2 + part) * 8
                    out[block * 2 + quad, x, part] = tiles[x][row : row + 8]


def x_forward_kernel(received, table, out, flat):
    for ky in range(8):
        pieces = []
        for block in range(8):
            first = received[block * 2, pl.ds(ky, 32, stride=8), :]
            second = received[block * 2 + 1, pl.ds(ky, 32, stride=8), :]
            pieces.append(first + second)
        values = table_dot(table[...], jnp.concatenate(pieces, 0))
        for part in range(2):
            flat[2 + part, ky * 32 : ky * 32 + 32] = values[part * 32 : part * 32 + 32]
    for part in range(2):
        for high in range(2):
            turned = flat[2 + part, high * 128 : high * 128 + 128].T
            tiles = swap_quads([turned[k * 32 : k * 32 + 32] for k in range(4)])
            for low in range(4):
                row = (high * 4 + low) * 32
                flat[part, row : row + 32] = tiles[low]
        for c in range(C):
            out[part, c] = flat[part, pl.ds(c, 8, stride=32), :]


def z_forward_rows_kernel(volume, table, out):
    lower = lax.broadcasted_iota(jnp.int32, (64, 128), 1) < 64
    for x in range(4):
        for half in range(2):
            block = volume[half * 16 : half * 16 + 16, x].reshape(256, Z)
            both = lax.dot_general(
                table[...], block, (((1,), (1,)), ((), ())), preferred_element_type=F32
            )
            values = both[:128] + both[128:]
            for pair in range(2):
                tile = values[:, pair * 128 : pair * 128 + 128]
                first, second = tile[:64], tile[64:]
                results = (
                    jnp.where(lower, first, pltpu.roll(second, 64, 1)),
                    jnp.where(lower, pltpu.roll(first, 64, 1), second),
                )
                for e in range(2):
                    target = half * 4 + pair * 2 + e
                    for part in range(2):
                        for group in range(4):
                            row = (part * 4 + group) * 8
                            out[target, group, x, part] = results[e][row : row + 8]


def x_forward_rows_kernel(received, table, out):
    for quad in range(2):
        columns = []
        for k in range(4):
            columns.append(
                jnp.concatenate(
                    [received[s, 0, pl.ds(quad * 4 + k, 32, stride=8), :] for s in range(8)], 0
                )
            )
        values = table_dot(table[...], jnp.concatenate(columns, 1))
        for pair in range(2):
            stack = [values[:, k * 128 : k * 128 + 128] for k in (2 * pair, 2 * pair + 1)]
            turned = jnp.concatenate(stack, 0).T
            for p in range(2):
                rows = [p * 64 + c * 16 for c in range(4)]
                tiles = swap_quads([turned[row : row + 16] for row in rows])
                for k in range(2):
                    for part in range(2):
                        out[p, 0, quad, 2 * pair + k, part] = tiles[2 * k + part]


def y_forward_rows_kernel(*refs):
    received, table, out = refs[:4], refs[4], refs[5]
    for target in range(4):
        columns = []
        for k in range(4):
            rows = slice(k * 32, k * 32 + 32)
            columns.append(jnp.concatenate([received[s][target, rows] for s in range(4)], 0))
        values = table_dot(table[...], jnp.concatenate(columns, 1))
        for k in range(4):
            out[target, k] = values[:, k * 128 : k * 128 + 128]


def sum_rows_kernel(place, *refs):
    received, out = refs[:4], refs[4]
    for target in range(8):
        offset = (target % 4 + 4 - place[1]) % 4 * 2 + (target // 4 + 2 - place[0]) % 2
        for k in range(4):
            rows = slice(target * 16, target * 16 + 16)
            total = (received[0][k, rows] + received[1][k, rows]) + (
                received[2][k, rows] + received[3][k, rows]
            )
            out[offset, k] = total.reshape(2, 8, 128)


def mix_kernel(weight, spectra, out):
    for o in range(0, 8, 4):
        rows = slice(o * 8, o * 8 + 32)

        def step(c, totals):
            real, imag = totals
            weight_real = weight[0, c, rows].astype(F32)
            weight_imag = weight[1, c, rows].astype(F32)
            field_real = jnp.concatenate([spectra[0, c]] * 4, 0)
            field_imag = jnp.concatenate([spectra[1, c]] * 4, 0)
            real = real + weight_real * field_real - weight_imag * field_imag
            imag = imag + weight_real * field_imag + weight_imag * field_real
            return real, imag

        zero = jnp.zeros((32, 128), F32)
        real, imag = lax.fori_loop(0, C, step, (zero, zero), unroll=4)
        out[0, rows] = real
        out[1, rows] = imag


def back_kernel(*refs):
    place, weight, mixed, partner = refs[:4]
    arrived, crossed, back, cotangent = refs[4:8], refs[8], refs[9], refs[10]
    factor = math.sqrt(X * Y * Z / (MX * MY * MZ))

    @pl.when(pl.program_id(0) == 0)
    def _():
        for part in range(2):
            for offset in range(8):
                i, j = offset // 2, offset % 2
                source = (place[0] + j) % 2 * 4 + (place[1] + 4 - i) % 4
                target = crossed.at[i] if j else arrived[i].at[0]
                tiles = swap_quads([target[k, part] for k in range(4)])
                for c in range(4):
                    rows = pl.ds(pl.multiple_of(source * 32 + c * 8, 8), 8)
                    cotangent[part, rows] = (0.5 * factor * factor) * (
                        mixed[part, rows] + partner[part, rows]
                    ) - factor * tiles[c]

    def step(c, carry):
        real = jnp.zeros((32, 128), F32)
        imag = jnp.zeros((32, 128), F32)
        for o in range(0, C, 4):
            rows = slice(o * 8, o * 8 + 32)
            weight_real = weight[0, c, rows].astype(F32)
            weight_imag = weight[1, c, rows].astype(F32)
            real = real + weight_real * cotangent[0, rows] + weight_imag * cotangent[1, rows]
            imag = imag + weight_real * cotangent[1, rows] - weight_imag * cotangent[0, rows]
        back[0, c] = real[:8] + real[8:16] + real[16:24] + real[24:]
        back[1, c] = imag[:8] + imag[8:16] + imag[16:24] + imag[24:]
        return carry

    lax.fori_loop(0, 8, step, 0)


def x_inverse_kernel(back, table, first, second, flat):
    for part in range(2):
        for c in range(C):
            flat[part, pl.ds(c, 8, stride=32), :] = back[part, c]
    for high in range(2):
        turned = []
        for part in range(2):
            rows = [(high * 4 + low) * 32 for low in range(4)]
            tiles = swap_quads([flat[part, row : row + 32] for row in rows])
            turned.append(jnp.concatenate(tiles, 0).T)
        for low in range(4):
            ky = high * 4 + low
            modes = jnp.concatenate([t[low * 32 : low * 32 + 32] for t in turned], 0)
            values = table_dot(table[...], modes)
            for block in range(8):
                row = block * 32
                for xl in range(2):
                    first[block * 2 + xl, pl.ds(ky, 16, stride=8), :] = values[row : row + 16]
                    second[block * 2 + xl, pl.ds(ky, 16, stride=8), :] = values[
                        row + 16 : row + 32
                    ]


def y_inverse_kernel(received, table, *out):
    for quad in range(2):
        tiles = []
        for x in range(4):
            tiles.append(
                jnp.concatenate(
                    [received[block * 2 + quad, x].reshape(16, 128) for block in range(8)], 0
                )
            )
        columns = swap_quads(tiles)
        values = table_dot(table[...], jnp.concatenate(columns, 1))
        for k in range(4):
            for target in range(8):
                out[target // 2][target % 2, 0, pl.ds(quad * 4 + k, 32, stride=8), :] = values[
                    target * 32 : target * 32 + 32, k * 128 : k * 128 + 128
                ]


def z_inverse_kernel(*refs):
    received, swap, table, out, rows = by_source(refs[:5]), *refs[5:7], *refs[-2:]
    for y in range(16):
        modes = jnp.concatenate([received[s][y].reshape(16, 128) for s in range(8)], 0)
        high, low = halves(modes.T)
        both = jnp.concatenate([high, low], 1)
        first = jnp.concatenate([table[:128], table[:128]], 0)
        values = dot(both, first) + dot(high, table[128:])
        rows[y] = values.astype(BF16).reshape(4, 32, Z)
    for x in range(4):
        for half in range(2):
            block = jnp.concatenate(
                [rows[y, x, half * 16 : half * 16 + 16, :] for y in range(16)], 0
            )
            moved = dot(swap[...], block).astype(BF16)
            out[half * 16 : half * 16 + 16, x] = moved.reshape(16, 16, Z)


SCALARS = pl.BlockSpec(memory_space=pltpu.SMEM)


def row_place():
    return jnp.stack([lax.axis_index("xh"), lax.axis_index("z")]).astype(jnp.int32)


def call(kernel, out, grid, in_specs, out_specs, scratch=(), cost=None, grant=40):
    return pl.pallas_call(
        kernel,
        out_shape=out,
        grid=grid,
        in_specs=in_specs,
        out_specs=out_specs,
        scratch_shapes=list(scratch),
        compiler_params=pltpu.CompilerParams(vmem_limit_bytes=grant * 2**20),
        cost_estimate=cost,
    )


def whole(*dims):
    return pl.BlockSpec(dims, lambda *i: (0,) * len(dims))


def struct(*dims, kind=F32):
    return jax.ShapeDtypeStruct(dims, kind)


def estimate(flops, moved):
    return pl.CostEstimate(flops=flops, bytes_accessed=moved, transcendentals=0)


def z_forward_call(volume, table):
    return call(
        z_forward_kernel,
        [struct(2, 4, 16, 2, 8, 128)] * 4,
        (4,),
        [
            pl.BlockSpec((32, 4, 16, Z), lambda i: (0, i, 0, 0)),
            whole(256, 256),
            whole(256, Z),
        ],
        [pl.BlockSpec((2, 1, 16, 2, 8, 128), lambda i: (0, i, 0, 0, 0, 0))] * 4,
        [pltpu.VMEM((16, 4, 32, Z), BF16)],
        estimate(3 * 2**30, 8 * 2**20),
        60,
    )(volume, jnp.asarray(swap_table()), table)


def y_forward_call(received, table):
    return call(
        y_forward_kernel,
        struct(16, 16, 2, 8, 128),
        (4,),
        [pl.BlockSpec((1, 1, 256, 128), lambda i: (0, i, 0, 0))] * 4
        + [pl.BlockSpec((4, 1, 256, 128), lambda i: (0, i, 0, 0)), whole(256, 256)],
        pl.BlockSpec((16, 4, 2, 8, 128), lambda i: (0, i, 0, 0, 0)),
        (),
        estimate(2 * 2**30, 6 * 2**20),
    )(*[block.reshape(block.shape[:-4] + (256, 128)) for block in received], table)


def z_forward_rows_call(volume, table):
    return call(
        z_forward_rows_kernel,
        struct(8, 4, 16, 2, 8, 128),
        (4,),
        [
            pl.BlockSpec((32, 4, 16, Z), lambda i: (0, i, 0, 0)),
            whole(256, Z),
        ],
        pl.BlockSpec((8, 4, 4, 2, 8, 128), lambda i: (0, 0, i, 0, 0, 0)),
        (),
        estimate(2 * 2**30, 8 * 2**20),
        60,
    )(volume, table)


def x_forward_rows_call(received):
    return call(
        x_forward_rows_kernel,
        struct(2, 4, 2, 4, 2, 16, 128),
        (4,),
        [
            pl.BlockSpec((8, 1, 256, 128), lambda i: (0, i, 0, 0)),
            whole(128, 256),
        ],
        pl.BlockSpec((2, 1, 2, 4, 2, 16, 128), lambda i: (0, i, 0, 0, 0, 0, 0)),
        (),
        estimate(2**20, 2**16),
    )(received.reshape(8, 4, 256, 128), jnp.asarray(stacked(x_forward())))


def y_forward_rows_call(received, table):
    return call(
        y_forward_rows_kernel,
        struct(4, 4, 128, 128),
        (),
        [whole(4, 128, 128)] * 4 + [whole(256, 128)],
        whole(4, 4, 128, 128),
        (),
        estimate(2**20, 2**16),
    )(*received, table)


def sum_rows_call(received):
    return call(
        sum_rows_kernel,
        struct(8, 4, 2, 8, 128),
        (),
        [SCALARS] + [whole(4, 128, 128)] * 4,
        whole(8, 4, 2, 8, 128),
        (),
        estimate(2**20, 2**16),
    )(row_place(), *received)


def x_forward_call(received):
    return call(
        x_forward_kernel,
        struct(2, 32, 8, 128),
        (),
        [whole(16, 256, 128), whole(128, 256)],
        whole(2, 32, 8, 128),
        [pltpu.VMEM((4, 256, 128), F32)],
        estimate(2**28, 3 * 2**20),
    )(received.reshape(16, 256, 128), jnp.asarray(stacked(x_forward())))


def mix_call(weight, spectra):
    return call(
        mix_kernel,
        struct(2, 256, 128),
        (4,),
        [
            pl.BlockSpec((2, 32, 64, 128), lambda i: (0, 0, i, 0)),
            whole(2, 32, 8, 128),
        ],
        pl.BlockSpec((2, 64, 128), lambda i: (0, i, 0)),
        (),
        estimate(2**27, 5 * 2**20),
    )(weight, spectra)


def back_call(weight, mixed, partner, target):
    small = whole(2, 256, 128)
    return call(
        back_kernel,
        (struct(2, 32, 8, 128), struct(2, 256, 128)),
        (4,),
        [
            SCALARS,
            pl.BlockSpec((2, 8, 256, 128), lambda i: (0, i, 0, 0)),
            small,
            small,
        ]
        + [whole(2, 4, 2, 8, 128)] * 4
        + [whole(4, 4, 2, 8, 128)],
        (pl.BlockSpec((2, 8, 8, 128), lambda i: (0, i, 0, 0)), small),
        (),
        estimate(2**27, 5 * 2**20),
    )(row_place(), weight, mixed, partner, *target)


def x_inverse_call(back):
    return call(
        x_inverse_kernel,
        [struct(16, 128, 128)] * 2,
        (),
        [whole(2, 32, 8, 128), whole(512, 64)],
        [whole(16, 128, 128)] * 2,
        [pltpu.VMEM((2, 256, 128), F32)],
        estimate(2**28, 3 * 2**20),
    )(back, jnp.asarray(stacked(x_inverse())))


def y_inverse_call(received, table):
    return call(
        y_inverse_kernel,
        [struct(2, 2, 256, 128)] * 4,
        (2,),
        [
            pl.BlockSpec((16, 4, 2, 8, 128), lambda i: (0, i, 0, 0, 0)),
            whole(512, 128),
        ],
        [pl.BlockSpec((2, 1, 256, 128), lambda i: (0, i, 0, 0))] * 4,
        (),
        estimate(2**30, 3 * 2**20),
    )(received.reshape(16, 8, 2, 8, 128), table)


def z_inverse_call(received, table, half, others):
    return pl.pallas_call(
        z_inverse_kernel,
        out_shape=struct(32, 16, 16, Z, kind=BF16),
        grid=(2,),
        in_specs=[pl.BlockSpec((1, 1, 16, 2, 8, 128), lambda i: (0, i, 0, 0, 0, 0))] * 4
        + [pl.BlockSpec((4, 1, 16, 2, 8, 128), lambda i: (0, i, 0, 0, 0, 0))]
        + [whole(256, 256), whole(256, Z)]
        + [pl.BlockSpec(memory_space=pl.ANY)] * len(others),
        out_specs=pl.BlockSpec((32, 4, 16, Z), lambda i: (0, i + 2 * half, 0, 0)),
        scratch_shapes=[pltpu.VMEM((16, 4, 32, Z), BF16)],
        input_output_aliases={7: 0} if others else {},
        compiler_params=pltpu.CompilerParams(vmem_limit_bytes=40 * 2**20),
        cost_estimate=estimate(3 * 2**29, 4 * 2**20),
    )(
        *[block.reshape(block.shape[:-2] + (16, 2, 8, 128)) for block in received],
        jnp.asarray(swap_table()),
        table,
        *others,
    )


def exchange(values, axes):
    return lax.all_to_all(values, axes, split_axis=0, concat_axis=0, tiled=True)


def offset_pairs(offset):
    index = np.arange(math.prod(SHAPE))
    place = np.stack(np.unravel_index(index, SHAPE))
    other = (place + np.array(offset)[:, None]) % np.array(SHAPE)[:, None]
    return list(zip(index.tolist(), np.ravel_multi_index(other, SHAPE).tolist()))


def shifted(values, **steps):
    offset = [steps.get(a, 0) for a in AXES]
    return lax.ppermute(values, AXES, offset_pairs(offset)) if any(offset) else values


def cross(arrived):
    return arrived + [shifted(jnp.stack([block[1] for block in arrived]), core=1)]


def by_place(build):
    tables = np.stack(
        [build(y, core, xl) for y in range(4) for core in range(2) for xl in range(2)]
    )
    y, core, xl = (lax.axis_index(a) for a in ("y", "core", "xl"))
    return lax.dynamic_index_in_dim(
        jnp.asarray(tables), (y * 2 + core) * 2 + xl, 0, keepdims=False
    )


def first_order(y, core, sign):
    return [((y + sign * i) % 4) * 2 + (core + sign * j) % 2 for i in range(4) for j in range(2)]


def z_rows_by_offset(y, core, xl):
    table = z_table().reshape(8, 16, Z)[first_order(y, core, 1)]
    return stacked(table.reshape(128, Z))


def z_rows_by_col(y, core, xl):
    order = [
        (((y + i) % 4) * 2 + (xl + j) % 2) * 2 + (core + k) % 2
        for i in range(4)
        for j in range(2)
        for k in range(2)
    ]
    return stacked(z_table_rows(order))


def y_columns_by_col(y, core, xl):
    return stacked(y_forward_rows([((y - i) % 4 * 2 + xl) * 2 + core for i in range(4)]))


def z_rows_by_source(y, core, xl):
    table = z_table().reshape(8, 16, Z)[first_order(y, core, -1)]
    return stacked(table.reshape(128, Z))


def y_rows_by_offset(y, core, xl):
    table = y_inverse(xl).reshape(8, 32, 128)[first_order(y, core, 1)]
    return stacked(table.reshape(256, 128))


def y_columns_by_offset(y, core, xl):
    table = y_forward(xl).reshape(128, 8, 32)[:, first_order(y, core, -1)]
    return stacked(table.reshape(128, 256))


def plane_pairs():
    index = np.arange(math.prod(SHAPE)).reshape(8, 16)[:, 0].tolist()
    same = [(index[b], index[7 - b]) for b in range(8)]
    edge = [(index[b], index[8 - b]) for b in range(1, 8)]
    return same, edge


def mirrored(mixed):
    same_pairs, edge_pairs = plane_pairs()
    plane = mixed.reshape(2, C, 8, 128)[..., :MX]
    same = lax.ppermute(plane, AXES, same_pairs)
    edge = lax.ppermute(plane[:, :, :1], AXES, edge_pairs)
    by_ky = jnp.concatenate([edge, same[:, :, :0:-1]], 2)
    by_kx = jnp.concatenate([jnp.zeros_like(by_ky[..., :1]), by_ky[..., :0:-1]], 3)
    signed = by_kx * jnp.array([1.0, -1.0], F32)[:, None, None, None]
    padded = jnp.pad(signed, ((0, 0),) * 3 + ((0, 128 - MX),))
    return padded.reshape(2, 256, 128)


def weight_grad(spectra, cotangent):
    real, imag = spectra.reshape(2, 1, C, 1, 8, 4, MX)
    turned = jnp.stack([cotangent[1], -cotangent[0]])
    cotangent, turned = (a.reshape(2, 1, C, 8, 4, MX) for a in (cotangent, turned))
    return (real * cotangent + imag * turned).astype(BF16)


def per_device(voxels, target, weight):
    barrier = lax.optimization_barrier
    packed = weight.reshape(2, C, 256, 128)

    target_lines = z_forward_rows_call(target, by_place(z_rows_by_col))
    target_lines, voxels = barrier((target_lines, voxels))
    target_lines = exchange(target_lines, ROW)
    lines = z_forward_call(voxels, by_place(z_rows_by_offset))
    lines = [shifted(block, y=i) for i, block in enumerate(lines)]
    target_lines, packed = barrier((target_lines, packed))
    blocks = x_forward_rows_call(target_lines).reshape(4, 4, 128, 128)
    lines, blocks = barrier((lines, blocks))
    blocks = [shifted(blocks[i], y=i) for i in range(4)]
    planes = y_forward_call(cross(lines), by_place(y_columns_by_offset))
    planes, blocks = barrier((planes, blocks))
    planes = exchange(planes, SECOND)
    blocks = y_forward_rows_call(blocks, by_place(y_columns_by_col))
    blocks = [shifted(blocks[2 * i + j], xl=i, core=j) for i in range(2) for j in range(2)]
    spectra = x_forward_call(planes)
    mixed = mix_call(packed, spectra)
    mixed, blocks = barrier((mixed, blocks))
    arrived = sum_rows_call(blocks)
    arrived = [shifted(arrived[2 * i : 2 * i + 2], z=i) for i in range(4)]
    partner, arrived = barrier((mirrored(mixed), arrived))
    crossed = shifted(jnp.stack([block[1] for block in arrived]), xh=1)
    back, cotangent = back_call(packed, mixed, partner, arrived + [crossed])
    y_table, z_table_here = by_place(y_rows_by_offset), by_place(z_rows_by_source)
    first, second = x_inverse_call(back)
    first, second = barrier((exchange(first, SECOND), second))
    first = y_inverse_call(first, y_table)
    first = [shifted(block, y=i) for i, block in enumerate(first)]
    second = y_inverse_call(exchange(second, SECOND), y_table)
    second = [shifted(block, y=i) for i, block in enumerate(second)]
    grad = weight_grad(spectra, cotangent)
    first, grad = barrier((first, grad))
    field = z_inverse_call(cross(first), z_table_here, 0, [])
    second, field = barrier((second, field))
    return z_inverse_call(cross(second), z_table_here, 1, [field]), grad


def solution(mesh):
    fine = Mesh(mesh.devices.reshape(SHAPE), AXES)
    field = P(None, ROW, COL, None)
    modes = P(None, None, None, ROW, COL, None)
    return jax.shard_map(
        per_device,
        mesh=fine,
        in_specs=(field, field, modes),
        out_specs=(field, modes),
        check_vma=False,
    )
```

```python
import functools
import math
import typing

import jax
import jax.numpy as jnp
import ml_dtypes
import numpy as np
from jax import lax
from jax.experimental import pallas as pl
from jax.experimental.pallas import tpu as pltpu
from jax.sharding import Mesh
from jax.sharding import PartitionSpec as P

C = 32
X = 128
Y = 256
Z = 256
MX = 32
MY = 64
MZ = 64

AXES = ("xh", "z", "y", "xl", "core")
SHAPE = (2, 4, 4, 2, 2)
ROW = ("xh", "z")
COL = ("y", "xl", "core")
FIRST = ("y", "core")
SECOND = ("xh", "z", "xl")
F32 = jnp.float32
BF16 = jnp.bfloat16


def split_parts(table):
    high = table.astype(ml_dtypes.bfloat16)
    low = (table - high.astype(np.float64)).astype(ml_dtypes.bfloat16)
    return high, low


def angles(frequency, position, length):
    return 2.0 * np.pi / length * ((frequency[:, None] * position[None, :]) % length)


def kept_z():
    y, core, part, xl, k = np.meshgrid(
        np.arange(4), np.arange(2), np.arange(2), np.arange(2), np.arange(4), indexing="ij"
    )
    return (((y * 2 + xl) * 2 + core) * 4 + k).reshape(-1), part.reshape(-1)


def z_table():
    frequency, part = kept_z()
    angle = angles(frequency, np.arange(Z), Z)
    return np.where(part[:, None] == 0, np.cos(angle), -np.sin(angle)) * Z**-0.5


def rotation(angle, row_part, column_part, sign):
    same = row_part[:, None] == column_part[None, :]
    lower = row_part[:, None] > column_part[None, :]
    return np.where(same, np.cos(angle), np.where(lower, sign, -sign) * np.sin(angle))


def y_points(xl):
    y, core, point, part = np.meshgrid(
        np.arange(4), np.arange(2), np.arange(16), np.arange(2), indexing="ij"
    )
    return (((y * 2 + xl) * 2 + core) * 16 + point).reshape(-1), part.reshape(-1)


def z_table_rows(order):
    half, part, place, k = np.meshgrid(
        np.arange(2), np.arange(2), np.arange(8), np.arange(4), indexing="ij"
    )
    frequency = np.array(order)[half * 8 + place] * 4 + k
    angle = angles(frequency.reshape(-1), np.arange(Z), Z)
    return np.where(part.reshape(-1, 1) == 0, np.cos(angle), -np.sin(angle)) * Z**-0.5


def y_forward_rows(places):
    block, part, point = np.meshgrid(
        np.array(places), np.arange(2), np.arange(16), indexing="ij"
    )
    frequency, row_part = y_modes()
    angle = angles(frequency, (block * 16 + point).reshape(-1), Y)
    return rotation(angle, row_part, part.reshape(-1), -1) * Y**-0.5


def y_modes():
    block, part, j = np.meshgrid(np.arange(8), np.arange(2), np.arange(8), indexing="ij")
    return (block * 8 + j).reshape(-1) - MY // 2, part.reshape(-1)


def y_forward(xl):
    position, column_part = y_points(xl)
    frequency, row_part = y_modes()
    return rotation(angles(frequency, position, Y), row_part, column_part, -1) * Y**-0.5


def y_inverse(xl):
    position, row_part = y_points(xl)
    frequency, column_part = y_modes()
    return rotation(angles(frequency, position, Y).T, row_part, column_part, 1) * Y**-0.5


def x_points():
    return np.repeat(np.arange(X), 2), np.tile(np.arange(2), X)


def x_modes():
    return np.tile(np.arange(MX), 2) - MX // 2, np.repeat(np.arange(2), MX)


def x_forward():
    position, column_part = x_points()
    frequency, row_part = x_modes()
    return rotation(angles(frequency, position, X), row_part, column_part, -1) * X**-0.5


def x_inverse():
    position, row_part = x_points()
    frequency, column_part = x_modes()
    return rotation(angles(frequency, position, X).T, row_part, column_part, 1) * X**-0.5


def stacked(table):
    return np.concatenate(split_parts(table), 0)


def swap_table():
    index = np.arange(256)
    table = np.zeros((256, 256), ml_dtypes.bfloat16)
    table[index, (index % 16) * 16 + index // 16] = 1
    return table


def dot(a, b):
    return jnp.dot(a, b, preferred_element_type=F32)


def halves(values):
    high = values.astype(BF16)
    return high, (values - high.astype(F32)).astype(BF16)


def table_dot(table, values):
    rows = table.shape[0] // 2
    high, low = halves(values)
    both = dot(table, high)
    return both[:rows] + both[rows:] + dot(table[:rows], low)


def swap_quads(tiles):
    lane = lax.broadcasted_iota(jnp.int32, tiles[0].shape, 1) // 32
    result = []
    for b in range(4):
        total = None
        for a in range(4):
            shift = (32 * (a - b)) % 128
            moved = pltpu.roll(tiles[a], shift, 1) if shift else tiles[a]
            total = moved if total is None else jnp.where(lane == a, moved, total)
        result.append(total)
    return result


def by_source(refs):
    crossed = refs[4]
    return [crossed.at[i, 0] if j else refs[i].at[0, 0] for i in range(4) for j in range(2)]


def z_forward_kernel(volume, swap, table, *refs):
    out, rows = refs[:4], refs[4]
    for x in range(4):
        for half in range(2):
            block = volume[half * 16 : half * 16 + 16, x].reshape(256, Z)
            moved = dot(swap[...], block).astype(BF16)
            for y in range(16):
                rows[y, x, half * 16 : half * 16 + 16, :] = moved[y * 16 : y * 16 + 16]
    for pair in range(8):
        points = rows[pair * 2 : pair * 2 + 2].reshape(256, Z)
        both = lax.dot_general(
            table[...], points, (((1,), (1,)), ((), ())), preferred_element_type=F32
        )
        values = both[:128] + both[128:]
        for y in range(2):
            for target in range(8):
                for part in range(2):
                    row = (target * 2 + part) * 8
                    out[target // 2][target % 2, 0, pair * 2 + y, part] = values[
                        row : row + 8, y * 128 : y * 128 + 128
                    ]


def y_forward_kernel(*refs):
    received, table, out = by_source(refs[:5]), refs[5], refs[6]
    for quad in range(2):
        columns = []
        for k in range(4):
            kz = quad * 4 + k
            columns.append(
                jnp.concatenate(
                    [received[s][pl.ds(kz, 32, stride=8), :] for s in range(8)], 0
                )
            )
        values = table_dot(table[...], jnp.concatenate(columns, 1))
        tiles = swap_quads([values[:, k * 128 : k * 128 + 128] for k in range(4)])
        for x in range(4):
            for block in range(8):
                for part in range(2):
                    row = (block * 2 + part) * 8
                    out[block * 2 + quad, x, part] = tiles[x][row : row + 8]


def x_forward_kernel(received, table, out, flat):
    for ky in range(8):
        pieces = []
        for block in range(8):
            first = received[block * 2, pl.ds(ky, 32, stride=8), :]
            second = received[block * 2 + 1, pl.ds(ky, 32, stride=8), :]
            pieces.append(first + second)
        values = table_dot(table[...], jnp.concatenate(pieces, 0))
        for part in range(2):
            flat[2 + part, ky * 32 : ky * 32 + 32] = values[part * 32 : part * 32 + 32]
    for part in range(2):
        for high in range(2):
            turned = flat[2 + part, high * 128 : high * 128 + 128].T
            tiles = swap_quads([turned[k * 32 : k * 32 + 32] for k in range(4)])
            for low in range(4):
                row = (high * 4 + low) * 32
                flat[part, row : row + 32] = tiles[low]
        for c in range(C):
            out[part, c] = flat[part, pl.ds(c, 8, stride=32), :]


def z_forward_rows_kernel(volume, table, out):
    lower = lax.broadcasted_iota(jnp.int32, (64, 128), 1) < 64
    for x in range(4):
        for half in range(2):
            block = volume[half * 16 : half * 16 + 16, x].reshape(256, Z)
            both = lax.dot_general(
                table[...], block, (((1,), (1,)), ((), ())), preferred_element_type=F32
            )
            values = both[:128] + both[128:]
            for pair in range(2):
                tile = values[:, pair * 128 : pair * 128 + 128]
                first, second = tile[:64], tile[64:]
                results = (
                    jnp.where(lower, first, pltpu.roll(second, 64, 1)),
                    jnp.where(lower, pltpu.roll(first, 64, 1), second),
                )
                for e in range(2):
                    target = half * 4 + pair * 2 + e
                    for part in range(2):
                        for group in range(4):
                            row = (part * 4 + group) * 8
                            out[target, group, x, part] = results[e][row : row + 8]


def x_forward_rows_kernel(received, table, out):
    for quad in range(2):
        columns = []
        for k in range(4):
            columns.append(
                jnp.concatenate(
                    [received[s, 0, pl.ds(quad * 4 + k, 32, stride=8), :] for s in range(8)], 0
                )
            )
        values = table_dot(table[...], jnp.concatenate(columns, 1))
        for pair in range(2):
            stack = [values[:, k * 128 : k * 128 + 128] for k in (2 * pair, 2 * pair + 1)]
            turned = jnp.concatenate(stack, 0).T
            for p in range(2):
                rows = [p * 64 + c * 16 for c in range(4)]
                tiles = swap_quads([turned[row : row + 16] for row in rows])
                for k in range(2):
                    for part in range(2):
                        out[p, 0, quad, 2 * pair + k, part] = tiles[2 * k + part]


def y_forward_rows_kernel(*refs):
    received, table, out = refs[:4], refs[4], refs[5]
    for target in range(4):
        columns = []
        for k in range(4):
            rows = slice(k * 32, k * 32 + 32)
            columns.append(jnp.concatenate([received[s][target, rows] for s in range(4)], 0))
        values = table_dot(table[...], jnp.concatenate(columns, 1))
        for k in range(4):
            out[target % 2, target // 2, k] = values[:, k * 128 : k * 128 + 128]


def sum_rows_kernel(place, *refs):
    received, out = refs[:2], refs[2]
    for target in range(8):
        offset = (target % 4 + 4 - place[1]) % 4 * 2 + (target // 4 + 2 - place[0]) % 2
        for k in range(4):
            rows = slice(target * 16, target * 16 + 16)
            total = received[0][k, rows] + received[1][k, rows]
            out[offset, k] = total.reshape(2, 8, 128)


def mix_kernel(weight, spectra, out):
    for o in range(0, 8, 4):
        rows = slice(o * 8, o * 8 + 32)

        def step(c, totals):
            real, imag = totals
            weight_real = weight[0, c, rows].astype(F32)
            weight_imag = weight[1, c, rows].astype(F32)
            field_real = jnp.concatenate([spectra[0, c]] * 4, 0)
            field_imag = jnp.concatenate([spectra[1, c]] * 4, 0)
            real = real + weight_real * field_real - weight_imag * field_imag
            imag = imag + weight_real * field_imag + weight_imag * field_real
            return real, imag

        zero = jnp.zeros((32, 128), F32)
        real, imag = lax.fori_loop(0, C, step, (zero, zero), unroll=4)
        out[0, rows] = real
        out[1, rows] = imag


def back_kernel(*refs):
    place, weight, mixed, partner = refs[:4]
    arrived, crossed, back, cotangent = refs[4:8], refs[8], refs[9], refs[10]
    factor = math.sqrt(X * Y * Z / (MX * MY * MZ))

    @pl.when(pl.program_id(0) == 0)
    def _():
        for part in range(2):
            for offset in range(8):
                i, j = offset // 2, offset % 2
                source = (place[0] + j) % 2 * 4 + (place[1] + 4 - i) % 4
                target = crossed.at[i] if j else arrived[i].at[0]
                tiles = swap_quads([target[k, part] for k in range(4)])
                for c in range(4):
                    rows = pl.ds(pl.multiple_of(source * 32 + c * 8, 8), 8)
                    cotangent[part, rows] = (0.5 * factor * factor) * (
                        mixed[part, rows] + partner[part, rows]
                    ) - factor * tiles[c]

    def step(c, carry):
        real = jnp.zeros((32, 128), F32)
        imag = jnp.zeros((32, 128), F32)
        for o in range(0, C, 4):
            rows = slice(o * 8, o * 8 + 32)
            weight_real = weight[0, c, rows].astype(F32)
            weight_imag = weight[1, c, rows].astype(F32)
            real = real + weight_real * cotangent[0, rows] + weight_imag * cotangent[1, rows]
            imag = imag + weight_real * cotangent[1, rows] - weight_imag * cotangent[0, rows]
        back[0, c] = real[:8] + real[8:16] + real[16:24] + real[24:]
        back[1, c] = imag[:8] + imag[8:16] + imag[16:24] + imag[24:]
        return carry

    lax.fori_loop(0, 8, step, 0)


def x_inverse_kernel(back, table, first, second, flat):
    for part in range(2):
        for c in range(C):
            flat[part, pl.ds(c, 8, stride=32), :] = back[part, c]
    for high in range(2):
        turned = []
        for part in range(2):
            rows = [(high * 4 + low) * 32 for low in range(4)]
            tiles = swap_quads([flat[part, row : row + 32] for row in rows])
            turned.append(jnp.concatenate(tiles, 0).T)
        for low in range(4):
            ky = high * 4 + low
            modes = jnp.concatenate([t[low * 32 : low * 32 + 32] for t in turned], 0)
            values = table_dot(table[...], modes)
            for block in range(8):
                row = block * 32
                for xl in range(2):
                    first[block * 2 + xl, pl.ds(ky, 16, stride=8), :] = values[row : row + 16]
                    second[block * 2 + xl, pl.ds(ky, 16, stride=8), :] = values[
                        row + 16 : row + 32
                    ]


def y_inverse_kernel(received, table, *out):
    for quad in range(2):
        tiles = []
        for x in range(4):
            tiles.append(
                jnp.concatenate(
                    [received[block * 2 + quad, x].reshape(16, 128) for block in range(8)], 0
                )
            )
        columns = swap_quads(tiles)
        values = table_dot(table[...], jnp.concatenate(columns, 1))
        for k in range(4):
            for target in range(8):
                out[target // 2][target % 2, 0, pl.ds(quad * 4 + k, 32, stride=8), :] = values[
                    target * 32 : target * 32 + 32, k * 128 : k * 128 + 128
                ]


def z_inverse_kernel(*refs):
    received, swap, table, out, rows = by_source(refs[:5]), *refs[5:7], *refs[-2:]
    for y in range(16):
        modes = jnp.concatenate([received[s][y].reshape(16, 128) for s in range(8)], 0)
        high, low = halves(modes.T)
        both = jnp.concatenate([high, low], 1)
        first = jnp.concatenate([table[:128], table[:128]], 0)
        values = dot(both, first) + dot(high, table[128:])
        rows[y] = values.astype(BF16).reshape(4, 32, Z)
    for x in range(4):
        for half in range(2):
            block = jnp.concatenate(
                [rows[y, x, half * 16 : half * 16 + 16, :] for y in range(16)], 0
            )
            moved = dot(swap[...], block).astype(BF16)
            out[half * 16 : half * 16 + 16, x] = moved.reshape(16, 16, Z)


SCALARS = pl.BlockSpec(memory_space=pltpu.SMEM)


def row_place():
    return jnp.stack([lax.axis_index("xh"), lax.axis_index("z")]).astype(jnp.int32)


def call(
    kernel, out, grid, in_specs, out_specs, scratch=(), cost=None, grant=40, place=None, aliases={}
):
    params = pltpu.CompilerParams(vmem_limit_bytes=grant * 2**20)
    if place is None:
        return pl.pallas_call(
            kernel,
            out_shape=out,
            grid=grid,
            in_specs=in_specs,
            out_specs=out_specs,
            scratch_shapes=list(scratch),
            compiler_params=params,
            cost_estimate=cost,
        )

    def fit(spec):
        if isinstance(spec, Placed):
            return pl.BlockSpec((None, spec.rows, spec.columns), lambda *a: (a[-1][0], 0, 0))
        if spec.index_map is None:
            return spec
        return pl.BlockSpec(spec.block_shape, lambda *a: spec.index_map(*a[:-1]))

    specs = [fit(spec) for spec in in_specs]
    single = isinstance(out_specs, pl.BlockSpec)
    built = pl.pallas_call(
        lambda index, *refs: kernel(*refs),
        out_shape=out,
        grid_spec=pltpu.PrefetchScalarGridSpec(
            num_scalar_prefetch=1,
            grid=grid or (1,),
            in_specs=specs,
            out_specs=fit(out_specs) if single else [fit(spec) for spec in out_specs],
            scratch_shapes=list(scratch),
        ),
        input_output_aliases=aliases,
        compiler_params=params,
        cost_estimate=cost,
    )
    return lambda *operands: built(place, *operands)


class Placed(typing.NamedTuple):
    rows: int
    columns: int


def whole(*dims):
    return pl.BlockSpec(dims, lambda *i: (0,) * len(dims))


def struct(*dims, kind=F32):
    return jax.ShapeDtypeStruct(dims, kind)


def estimate(flops, moved):
    return pl.CostEstimate(flops=flops, bytes_accessed=moved, transcendentals=0)


def z_forward_call(volume, table):
    return call(
        z_forward_kernel,
        [struct(2, 4, 16, 2, 8, 128)] * 4,
        (4,),
        [
            pl.BlockSpec((32, 4, 16, Z), lambda i: (0, i, 0, 0)),
            whole(256, 256),
            Placed(256, Z),
        ],
        [pl.BlockSpec((2, 1, 16, 2, 8, 128), lambda i: (0, i, 0, 0, 0, 0))] * 4,
        [pltpu.VMEM((16, 4, 32, Z), BF16)],
        estimate(3 * 2**30, 8 * 2**20),
        60,
        own_place(),
    )(volume, jnp.asarray(swap_table()), table)


def y_forward_call(received, table):
    return call(
        y_forward_kernel,
        struct(16, 16, 2, 8, 128),
        (4,),
        [pl.BlockSpec((1, 1, 256, 128), lambda i: (0, i, 0, 0))] * 4
        + [pl.BlockSpec((4, 1, 256, 128), lambda i: (0, i, 0, 0)), Placed(256, 256)],
        pl.BlockSpec((16, 4, 2, 8, 128), lambda i: (0, i, 0, 0, 0)),
        (),
        estimate(2 * 2**30, 6 * 2**20),
        place=own_place(),
    )(*[block.reshape(block.shape[:-4] + (256, 128)) for block in received], table)


def z_forward_rows_call(volume, table):
    return call(
        z_forward_rows_kernel,
        struct(8, 4, 16, 2, 8, 128),
        (4,),
        [
            pl.BlockSpec((32, 4, 16, Z), lambda i: (0, i, 0, 0)),
            Placed(256, Z),
        ],
        pl.BlockSpec((8, 4, 4, 2, 8, 128), lambda i: (0, 0, i, 0, 0, 0)),
        (),
        estimate(2 * 2**30, 8 * 2**20),
        60,
        own_place(),
    )(volume, table)


def x_forward_rows_call(received):
    return call(
        x_forward_rows_kernel,
        struct(2, 4, 2, 4, 2, 16, 128),
        (4,),
        [
            pl.BlockSpec((8, 1, 256, 128), lambda i: (0, i, 0, 0)),
            whole(128, 256),
        ],
        pl.BlockSpec((2, 1, 2, 4, 2, 16, 128), lambda i: (0, i, 0, 0, 0, 0, 0)),
        (),
        estimate(2**20, 2**16),
    )(received.reshape(8, 4, 256, 128), jnp.asarray(stacked(x_forward())))


def y_forward_rows_call(received, table):
    return call(
        y_forward_rows_kernel,
        struct(2, 2, 4, 128, 128),
        (),
        [whole(4, 128, 128)] * 4 + [Placed(256, 128)],
        whole(2, 2, 4, 128, 128),
        (),
        estimate(2**20, 2**16),
        place=own_place(),
    )(*received, table)


def sum_rows_call(received):
    return call(
        sum_rows_kernel,
        struct(8, 4, 2, 8, 128),
        (),
        [SCALARS] + [whole(4, 128, 128)] * 2,
        whole(8, 4, 2, 8, 128),
        (),
        estimate(2**20, 2**16),
    )(row_place(), *received)


def x_forward_call(received):
    return call(
        x_forward_kernel,
        struct(2, 32, 8, 128),
        (),
        [whole(16, 256, 128), whole(128, 256)],
        whole(2, 32, 8, 128),
        [pltpu.VMEM((4, 256, 128), F32)],
        estimate(2**28, 3 * 2**20),
    )(received.reshape(16, 256, 128), jnp.asarray(stacked(x_forward())))


def mix_call(weight, spectra):
    return call(
        mix_kernel,
        struct(2, 256, 128),
        (4,),
        [
            pl.BlockSpec((2, 32, 64, 128), lambda i: (0, 0, i, 0)),
            whole(2, 32, 8, 128),
        ],
        pl.BlockSpec((2, 64, 128), lambda i: (0, i, 0)),
        (),
        estimate(2**27, 5 * 2**20),
    )(weight, spectra)


def back_call(weight, mixed, partner, target):
    small = whole(2, 256, 128)
    return call(
        back_kernel,
        (struct(2, 32, 8, 128), struct(2, 256, 128)),
        (4,),
        [
            SCALARS,
            pl.BlockSpec((2, 8, 256, 128), lambda i: (0, i, 0, 0)),
            small,
            small,
        ]
        + [whole(2, 4, 2, 8, 128)] * 4
        + [whole(4, 4, 2, 8, 128)],
        (pl.BlockSpec((2, 8, 8, 128), lambda i: (0, i, 0, 0)), small),
        (),
        estimate(2**27, 5 * 2**20),
    )(row_place(), weight, mixed, partner, *target)


def x_inverse_call(back):
    return call(
        x_inverse_kernel,
        [struct(16, 128, 128)] * 2,
        (),
        [whole(2, 32, 8, 128), whole(512, 64)],
        [whole(16, 128, 128)] * 2,
        [pltpu.VMEM((2, 256, 128), F32)],
        estimate(2**28, 3 * 2**20),
    )(back, jnp.asarray(stacked(x_inverse())))


def y_inverse_call(received, table):
    return call(
        y_inverse_kernel,
        [struct(2, 2, 256, 128)] * 4,
        (2,),
        [
            pl.BlockSpec((16, 4, 2, 8, 128), lambda i: (0, i, 0, 0, 0)),
            Placed(512, 128),
        ],
        [pl.BlockSpec((2, 1, 256, 128), lambda i: (0, i, 0, 0))] * 4,
        (),
        estimate(2**30, 3 * 2**20),
        place=own_place(),
    )(received.reshape(16, 8, 2, 8, 128), table)


def z_inverse_call(received, table, half, others):
    return call(
        z_inverse_kernel,
        struct(32, 16, 16, Z, kind=BF16),
        (2,),
        [pl.BlockSpec((1, 1, 16, 2, 8, 128), lambda i: (0, i, 0, 0, 0, 0))] * 4
        + [pl.BlockSpec((4, 1, 16, 2, 8, 128), lambda i: (0, i, 0, 0, 0, 0))]
        + [whole(256, 256), Placed(256, Z)]
        + [pl.BlockSpec(memory_space=pl.ANY)] * len(others),
        pl.BlockSpec((32, 4, 16, Z), lambda i: (0, i + 2 * half, 0, 0)),
        [pltpu.VMEM((16, 4, 32, Z), BF16)],
        estimate(3 * 2**29, 4 * 2**20),
        place=own_place(),
        aliases={8: 0} if others else {},
    )(
        *[block.reshape(block.shape[:-2] + (16, 2, 8, 128)) for block in received],
        jnp.asarray(swap_table()),
        table,
        *others,
    )


def exchange(values, axes):
    return lax.all_to_all(values, axes, split_axis=0, concat_axis=0, tiled=True)


def offset_pairs(offset):
    index = np.arange(math.prod(SHAPE))
    place = np.stack(np.unravel_index(index, SHAPE))
    other = (place + np.array(offset)[:, None]) % np.array(SHAPE)[:, None]
    return list(zip(index.tolist(), np.ravel_multi_index(other, SHAPE).tolist()))


def shifted(values, **steps):
    offset = [steps.get(a, 0) for a in AXES]
    return lax.ppermute(values, AXES, offset_pairs(offset)) if any(offset) else values


def cross(arrived):
    return arrived + [shifted(jnp.stack([block[1] for block in arrived]), core=1)]


def by_place(build):
    return jnp.asarray(
        np.stack([build(y, core, xl) for y in range(4) for core in range(2) for xl in range(2)])
    )


def own_place():
    y, core, xl = (lax.axis_index(a) for a in ("y", "core", "xl"))
    return ((y * 2 + core) * 2 + xl).astype(jnp.int32).reshape(1)


def first_order(y, core, sign):
    return [((y + sign * i) % 4) * 2 + (core + sign * j) % 2 for i in range(4) for j in range(2)]


def z_rows_by_offset(y, core, xl):
    table = z_table().reshape(8, 16, Z)[first_order(y, core, 1)]
    return stacked(table.reshape(128, Z))


def z_rows_by_col(y, core, xl):
    order = [
        (((y + i) % 4) * 2 + (xl + j) % 2) * 2 + (core + k) % 2
        for i in range(4)
        for j in range(2)
        for k in range(2)
    ]
    return stacked(z_table_rows(order))


def y_columns_by_col(y, core, xl):
    return stacked(y_forward_rows([((y - i) % 4 * 2 + xl) * 2 + core for i in range(4)]))


def z_rows_by_source(y, core, xl):
    table = z_table().reshape(8, 16, Z)[first_order(y, core, -1)]
    return stacked(table.reshape(128, Z))


def y_rows_by_offset(y, core, xl):
    table = y_inverse(xl).reshape(8, 32, 128)[first_order(y, core, 1)]
    return stacked(table.reshape(256, 128))


def y_columns_by_offset(y, core, xl):
    table = y_forward(xl).reshape(128, 8, 32)[:, first_order(y, core, -1)]
    return stacked(table.reshape(128, 256))


def plane_pairs():
    index = np.arange(math.prod(SHAPE)).reshape(8, 16)[:, 0].tolist()
    same = [(index[b], index[7 - b]) for b in range(8)]
    edge = [(index[b], index[8 - b]) for b in range(1, 8)]
    return same, edge


def mirrored(mixed):
    same_pairs, edge_pairs = plane_pairs()
    plane = mixed.reshape(2, C, 8, 128)[..., :MX]
    same = lax.ppermute(plane, AXES, same_pairs)
    edge = lax.ppermute(plane[:, :, :1], AXES, edge_pairs)
    by_ky = jnp.concatenate([edge, same[:, :, :0:-1]], 2)
    by_kx = jnp.concatenate([jnp.zeros_like(by_ky[..., :1]), by_ky[..., :0:-1]], 3)
    signed = by_kx * jnp.array([1.0, -1.0], F32)[:, None, None, None]
    padded = jnp.pad(signed, ((0, 0),) * 3 + ((0, 128 - MX),))
    return padded.reshape(2, 256, 128)


def weight_grad(spectra, cotangent):
    real, imag = spectra.reshape(2, 1, C, 1, 8, 4, MX)
    turned = jnp.stack([cotangent[1], -cotangent[0]])
    cotangent, turned = (a.reshape(2, 1, C, 8, 4, MX) for a in (cotangent, turned))
    return (real * cotangent + imag * turned).astype(BF16)


def per_device(voxels, target, weight):
    barrier = lax.optimization_barrier
    packed = weight.reshape(2, C, 256, 128)

    target_lines = z_forward_rows_call(target, by_place(z_rows_by_col))
    target_lines, voxels = barrier((target_lines, voxels))
    target_lines = exchange(target_lines, ROW)
    lines = z_forward_call(voxels, by_place(z_rows_by_offset))
    lines = [shifted(block, y=i) for i, block in enumerate(lines)]
    target_lines, packed = barrier((target_lines, packed))
    blocks = x_forward_rows_call(target_lines).reshape(4, 4, 128, 128)
    lines, blocks = barrier((lines, blocks))
    blocks = [shifted(blocks[i], y=i) for i in range(4)]
    planes = y_forward_call(cross(lines), by_place(y_columns_by_offset))
    planes = exchange(planes, SECOND)
    blocks = y_forward_rows_call(blocks, by_place(y_columns_by_col))
    blocks = blocks[0] + shifted(blocks[1], core=1)
    blocks = [blocks[0], shifted(blocks[1], xl=1)]
    spectra = x_forward_call(planes)
    mixed = mix_call(packed, spectra)
    mixed, blocks = barrier((mixed, blocks))
    mixed, sums = barrier((mixed, sum_rows_call(blocks)))
    arrived = [shifted(sums[2 * i : 2 * i + 2], z=i) for i in range(4)]
    partner = mirrored(mixed)
    partner, arrived = barrier((partner, arrived))
    crossed = shifted(jnp.stack([block[1] for block in arrived]), xh=1)
    back, cotangent = back_call(packed, mixed, partner, arrived + [crossed])
    y_table, z_table_here = by_place(y_rows_by_offset), by_place(z_rows_by_source)
    first, second = x_inverse_call(back)
    first, second = barrier((exchange(first, SECOND), second))
    first = y_inverse_call(first, y_table)
    first = [shifted(block, y=i) for i, block in enumerate(first)]
    second = y_inverse_call(exchange(second, SECOND), y_table)
    first, second = barrier((first, second))
    second = [shifted(block, y=i) for i, block in enumerate(second)]
    grad = weight_grad(spectra, cotangent)
    first, grad = barrier((first, grad))
    field = z_inverse_call(cross(first), z_table_here, 0, [])
    second, field = barrier((second, field))
    return z_inverse_call(cross(second), z_table_here, 1, [field]), grad


def solution(mesh):
    fine = Mesh(mesh.devices.reshape(SHAPE), AXES)
    field = P(None, ROW, COL, None)
    modes = P(None, None, None, ROW, COL, None)
    return jax.shard_map(
        per_device,
        mesh=fine,
        in_specs=(field, field, modes),
        out_specs=(field, modes),
        check_vma=False,
    )
```

```python
import functools
import math
import typing

import jax
import jax.numpy as jnp
import ml_dtypes
import numpy as np
from jax import lax
from jax.experimental import pallas as pl
from jax.experimental.pallas import tpu as pltpu
from jax.sharding import Mesh
from jax.sharding import PartitionSpec as P

C = 32
X = 128
Y = 256
Z = 256
MX = 32
MY = 64
MZ = 64

AXES = ("xh", "z", "y", "xl", "core")
SHAPE = (2, 4, 4, 2, 2)
ROW = ("xh", "z")
COL = ("y", "xl", "core")
FIRST = ("y", "core")
SECOND = ("xh", "z", "xl")
F32 = jnp.float32
BF16 = jnp.bfloat16


def split_parts(table):
    high = table.astype(ml_dtypes.bfloat16)
    low = (table - high.astype(np.float64)).astype(ml_dtypes.bfloat16)
    return high, low


def angles(frequency, position, length):
    return 2.0 * np.pi / length * ((frequency[:, None] * position[None, :]) % length)


def kept_z():
    y, core, part, xl, k = np.meshgrid(
        np.arange(4), np.arange(2), np.arange(2), np.arange(2), np.arange(4), indexing="ij"
    )
    return (((y * 2 + xl) * 2 + core) * 4 + k).reshape(-1), part.reshape(-1)


def z_table():
    frequency, part = kept_z()
    angle = angles(frequency, np.arange(Z), Z)
    return np.where(part[:, None] == 0, np.cos(angle), -np.sin(angle)) * Z**-0.5


def rotation(angle, row_part, column_part, sign):
    same = row_part[:, None] == column_part[None, :]
    lower = row_part[:, None] > column_part[None, :]
    return np.where(same, np.cos(angle), np.where(lower, sign, -sign) * np.sin(angle))


def y_points(xl):
    y, core, point, part = np.meshgrid(
        np.arange(4), np.arange(2), np.arange(16), np.arange(2), indexing="ij"
    )
    return (((y * 2 + xl) * 2 + core) * 16 + point).reshape(-1), part.reshape(-1)


def z_table_rows(order):
    half, part, place, k = np.meshgrid(
        np.arange(2), np.arange(2), np.arange(8), np.arange(4), indexing="ij"
    )
    frequency = np.array(order)[half * 8 + place] * 4 + k
    angle = angles(frequency.reshape(-1), np.arange(Z), Z)
    return np.where(part.reshape(-1, 1) == 0, np.cos(angle), -np.sin(angle)) * Z**-0.5


def y_forward_rows(places):
    block, part, point = np.meshgrid(
        np.array(places), np.arange(2), np.arange(16), indexing="ij"
    )
    frequency, row_part = y_modes()
    angle = angles(frequency, (block * 16 + point).reshape(-1), Y)
    return rotation(angle, row_part, part.reshape(-1), -1) * Y**-0.5


def y_modes():
    block, part, j = np.meshgrid(np.arange(8), np.arange(2), np.arange(8), indexing="ij")
    return (block * 8 + j).reshape(-1) - MY // 2, part.reshape(-1)


def y_forward(xl):
    position, column_part = y_points(xl)
    frequency, row_part = y_modes()
    return rotation(angles(frequency, position, Y), row_part, column_part, -1) * Y**-0.5


def y_inverse(xl):
    position, row_part = y_points(xl)
    frequency, column_part = y_modes()
    return rotation(angles(frequency, position, Y).T, row_part, column_part, 1) * Y**-0.5


def x_points():
    return np.repeat(np.arange(X), 2), np.tile(np.arange(2), X)


def x_modes():
    return np.tile(np.arange(MX), 2) - MX // 2, np.repeat(np.arange(2), MX)


def x_forward():
    position, column_part = x_points()
    frequency, row_part = x_modes()
    return rotation(angles(frequency, position, X), row_part, column_part, -1) * X**-0.5


def x_inverse():
    position, row_part = x_points()
    frequency, column_part = x_modes()
    return rotation(angles(frequency, position, X).T, row_part, column_part, 1) * X**-0.5


def stacked(table):
    return np.concatenate(split_parts(table), 0)


def swap_table():
    index = np.arange(256)
    table = np.zeros((256, 256), ml_dtypes.bfloat16)
    table[index, (index % 16) * 16 + index // 16] = 1
    return table


def dot(a, b):
    return jnp.dot(a, b, preferred_element_type=F32)


def halves(values):
    high = values.astype(BF16)
    return high, (values - high.astype(F32)).astype(BF16)


def table_dot(table, values):
    rows = table.shape[0] // 2
    high, low = halves(values)
    both = dot(table, high)
    return both[:rows] + both[rows:] + dot(table[:rows], low)


def swap_quads(tiles):
    lane = lax.broadcasted_iota(jnp.int32, tiles[0].shape, 1) // 32
    result = []
    for b in range(4):
        total = None
        for a in range(4):
            shift = (32 * (a - b)) % 128
            moved = pltpu.roll(tiles[a], shift, 1) if shift else tiles[a]
            total = moved if total is None else jnp.where(lane == a, moved, total)
        result.append(total)
    return result


def by_source(refs):
    crossed = refs[4]
    return [crossed.at[i, 0] if j else refs[i].at[0, 0] for i in range(4) for j in range(2)]


def z_forward_kernel(volume, swap, table, *refs):
    out, rows = refs[:4], refs[4]
    for x in range(4):
        for half in range(2):
            block = volume[half * 16 : half * 16 + 16, x].reshape(256, Z)
            moved = dot(swap[...], block).astype(BF16)
            for y in range(16):
                rows[y, x, half * 16 : half * 16 + 16, :] = moved[y * 16 : y * 16 + 16]
    for pair in range(8):
        points = rows[pair * 2 : pair * 2 + 2].reshape(256, Z)
        both = lax.dot_general(
            table[...], points, (((1,), (1,)), ((), ())), preferred_element_type=F32
        )
        values = both[:128] + both[128:]
        for y in range(2):
            for target in range(8):
                for part in range(2):
                    row = (target * 2 + part) * 8
                    out[target // 2][target % 2, 0, pair * 2 + y, part] = values[
                        row : row + 8, y * 128 : y * 128 + 128
                    ]


def y_forward_kernel(*refs):
    received, table, out = by_source(refs[:5]), refs[5], refs[6]
    for quad in range(2):
        columns = []
        for k in range(4):
            kz = quad * 4 + k
            columns.append(
                jnp.concatenate(
                    [received[s][pl.ds(kz, 32, stride=8), :] for s in range(8)], 0
                )
            )
        values = table_dot(table[...], jnp.concatenate(columns, 1))
        tiles = swap_quads([values[:, k * 128 : k * 128 + 128] for k in range(4)])
        for x in range(4):
            for block in range(8):
                for part in range(2):
                    row = (block * 2 + part) * 8
                    out[block * 2 + quad, x, part] = tiles[x][row : row + 8]


def x_forward_kernel(received, table, out, flat):
    for ky in range(8):
        pieces = []
        for block in range(8):
            first = received[block * 2, pl.ds(ky, 32, stride=8), :]
            second = received[block * 2 + 1, pl.ds(ky, 32, stride=8), :]
            pieces.append(first + second)
        values = table_dot(table[...], jnp.concatenate(pieces, 0))
        for part in range(2):
            flat[2 + part, ky * 32 : ky * 32 + 32] = values[part * 32 : part * 32 + 32]
    for part in range(2):
        for high in range(2):
            turned = flat[2 + part, high * 128 : high * 128 + 128].T
            tiles = swap_quads([turned[k * 32 : k * 32 + 32] for k in range(4)])
            for low in range(4):
                row = (high * 4 + low) * 32
                flat[part, row : row + 32] = tiles[low]
        for c in range(C):
            out[part, c] = flat[part, pl.ds(c, 8, stride=32), :]


def z_forward_rows_kernel(volume, table, out):
    lower = lax.broadcasted_iota(jnp.int32, (64, 128), 1) < 64
    for x in range(4):
        for half in range(2):
            block = volume[half * 16 : half * 16 + 16, x].reshape(256, Z)
            both = lax.dot_general(
                table[...], block, (((1,), (1,)), ((), ())), preferred_element_type=F32
            )
            values = both[:128] + both[128:]
            for pair in range(2):
                tile = values[:, pair * 128 : pair * 128 + 128]
                first, second = tile[:64], tile[64:]
                results = (
                    jnp.where(lower, first, pltpu.roll(second, 64, 1)),
                    jnp.where(lower, pltpu.roll(first, 64, 1), second),
                )
                for e in range(2):
                    target = half * 4 + pair * 2 + e
                    for part in range(2):
                        for group in range(4):
                            row = (part * 4 + group) * 8
                            out[target, group, x, part] = results[e][row : row + 8]


def x_forward_rows_kernel(received, table, out):
    for quad in range(2):
        columns = []
        for k in range(4):
            columns.append(
                jnp.concatenate(
                    [received[s, 0, pl.ds(quad * 4 + k, 32, stride=8), :] for s in range(8)], 0
                )
            )
        values = table_dot(table[...], jnp.concatenate(columns, 1))
        for pair in range(2):
            stack = [values[:, k * 128 : k * 128 + 128] for k in (2 * pair, 2 * pair + 1)]
            turned = jnp.concatenate(stack, 0).T
            for p in range(2):
                rows = [p * 64 + c * 16 for c in range(4)]
                tiles = swap_quads([turned[row : row + 16] for row in rows])
                for k in range(2):
                    for part in range(2):
                        out[p, 0, quad, 2 * pair + k, part] = tiles[2 * k + part]


def y_forward_rows_kernel(*refs):
    received, table, out = refs[:4], refs[4], refs[5]
    for target in range(4):
        columns = []
        for k in range(4):
            rows = slice(k * 32, k * 32 + 32)
            columns.append(jnp.concatenate([received[s][target, rows] for s in range(4)], 0))
        values = table_dot(table[...], jnp.concatenate(columns, 1))
        for k in range(4):
            out[target % 2, target // 2, k] = values[:, k * 128 : k * 128 + 128]


def sum_rows_kernel(place, *refs):
    received, out = refs[:2], refs[2]
    for target in range(8):
        offset = (target % 4 + 4 - place[1]) % 4 * 2 + (target // 4 + 2 - place[0]) % 2
        for k in range(4):
            rows = slice(target * 16, target * 16 + 16)
            total = received[0][k, rows] + received[1][k, rows]
            out[offset, k] = total.reshape(2, 8, 128)


def mix_kernel(weight, spectra, out):
    for o in range(0, 8, 4):
        rows = slice(o * 8, o * 8 + 32)

        def step(c, totals):
            real, imag = totals
            weight_real = weight[0, c, rows].astype(F32)
            weight_imag = weight[1, c, rows].astype(F32)
            field_real = jnp.concatenate([spectra[0, c]] * 4, 0)
            field_imag = jnp.concatenate([spectra[1, c]] * 4, 0)
            real = real + weight_real * field_real - weight_imag * field_imag
            imag = imag + weight_real * field_imag + weight_imag * field_real
            return real, imag

        zero = jnp.zeros((32, 128), F32)
        real, imag = lax.fori_loop(0, C, step, (zero, zero), unroll=4)
        out[0, rows] = real
        out[1, rows] = imag


def back_kernel(*refs):
    place, weight, mixed, partner = refs[:4]
    arrived, crossed, back, cotangent = refs[4:8], refs[8], refs[9], refs[10]
    factor = math.sqrt(X * Y * Z / (MX * MY * MZ))

    @pl.when(pl.program_id(0) == 0)
    def _():
        for part in range(2):
            for offset in range(8):
                i, j = offset // 2, offset % 2
                source = (place[0] + j) % 2 * 4 + (place[1] + 4 - i) % 4
                target = crossed.at[i] if j else arrived[i].at[0]
                tiles = swap_quads([target[k, part] for k in range(4)])
                for c in range(4):
                    rows = pl.ds(pl.multiple_of(source * 32 + c * 8, 8), 8)
                    cotangent[part, rows] = (0.5 * factor * factor) * (
                        mixed[part, rows] + partner[part, rows]
                    ) - factor * tiles[c]

    def step(c, carry):
        real = jnp.zeros((32, 128), F32)
        imag = jnp.zeros((32, 128), F32)
        for o in range(0, C, 4):
            rows = slice(o * 8, o * 8 + 32)
            weight_real = weight[0, c, rows].astype(F32)
            weight_imag = weight[1, c, rows].astype(F32)
            real = real + weight_real * cotangent[0, rows] + weight_imag * cotangent[1, rows]
            imag = imag + weight_real * cotangent[1, rows] - weight_imag * cotangent[0, rows]
        back[0, c] = real[:8] + real[8:16] + real[16:24] + real[24:]
        back[1, c] = imag[:8] + imag[8:16] + imag[16:24] + imag[24:]
        return carry

    lax.fori_loop(0, 8, step, 0)


def x_inverse_kernel(back, table, first, second, flat):
    for part in range(2):
        for c in range(C):
            flat[part, pl.ds(c, 8, stride=32), :] = back[part, c]
    for high in range(2):
        turned = []
        for part in range(2):
            rows = [(high * 4 + low) * 32 for low in range(4)]
            tiles = swap_quads([flat[part, row : row + 32] for row in rows])
            turned.append(jnp.concatenate(tiles, 0).T)
        for low in range(4):
            ky = high * 4 + low
            modes = jnp.concatenate([t[low * 32 : low * 32 + 32] for t in turned], 0)
            values = table_dot(table[...], modes)
            for block in range(8):
                row = block * 32
                for xl in range(2):
                    first[block * 2 + xl, pl.ds(ky, 16, stride=8), :] = values[row : row + 16]
                    second[block * 2 + xl, pl.ds(ky, 16, stride=8), :] = values[
                        row + 16 : row + 32
                    ]


def y_inverse_kernel(received, table, *out):
    for quad in range(2):
        tiles = []
        for x in range(4):
            tiles.append(
                jnp.concatenate(
                    [received[block * 2 + quad, x].reshape(16, 128) for block in range(8)], 0
                )
            )
        columns = swap_quads(tiles)
        values = table_dot(table[...], jnp.concatenate(columns, 1))
        for k in range(4):
            for target in range(8):
                out[target // 2][target % 2, 0, pl.ds(quad * 4 + k, 32, stride=8), :] = values[
                    target * 32 : target * 32 + 32, k * 128 : k * 128 + 128
                ]


def z_inverse_kernel(*refs):
    received, swap, table, out, rows = by_source(refs[:5]), *refs[5:7], *refs[-2:]
    for y in range(16):
        modes = jnp.concatenate([received[s][y].reshape(16, 128) for s in range(8)], 0)
        high, low = halves(modes.T)
        both = jnp.concatenate([high, low], 1)
        first = jnp.concatenate([table[:128], table[:128]], 0)
        values = dot(both, first) + dot(high, table[128:])
        rows[y] = values.astype(BF16).reshape(4, 32, Z)
    for x in range(4):
        for half in range(2):
            block = jnp.concatenate(
                [rows[y, x, half * 16 : half * 16 + 16, :] for y in range(16)], 0
            )
            moved = dot(swap[...], block).astype(BF16)
            out[half * 16 : half * 16 + 16, x] = moved.reshape(16, 16, Z)


SCALARS = pl.BlockSpec(memory_space=pltpu.SMEM)


def row_place():
    return jnp.stack([lax.axis_index("xh"), lax.axis_index("z")]).astype(jnp.int32)


def call(
    kernel, out, grid, in_specs, out_specs, scratch=(), cost=None, grant=40, place=None, aliases={}
):
    params = pltpu.CompilerParams(vmem_limit_bytes=grant * 2**20)
    if place is None:
        return pl.pallas_call(
            kernel,
            out_shape=out,
            grid=grid,
            in_specs=in_specs,
            out_specs=out_specs,
            scratch_shapes=list(scratch),
            compiler_params=params,
            cost_estimate=cost,
        )

    def fit(spec):
        if isinstance(spec, Placed):
            return pl.BlockSpec((None, spec.rows, spec.columns), lambda *a: (a[-1][0], 0, 0))
        if spec.index_map is None:
            return spec
        return pl.BlockSpec(spec.block_shape, lambda *a: spec.index_map(*a[:-1]))

    specs = [fit(spec) for spec in in_specs]
    single = isinstance(out_specs, pl.BlockSpec)
    built = pl.pallas_call(
        lambda index, *refs: kernel(*refs),
        out_shape=out,
        grid_spec=pltpu.PrefetchScalarGridSpec(
            num_scalar_prefetch=1,
            grid=grid or (1,),
            in_specs=specs,
            out_specs=fit(out_specs) if single else [fit(spec) for spec in out_specs],
            scratch_shapes=list(scratch),
        ),
        input_output_aliases=aliases,
        compiler_params=params,
        cost_estimate=cost,
    )
    return lambda *operands: built(place, *operands)


class Placed(typing.NamedTuple):
    rows: int
    columns: int


def whole(*dims):
    return pl.BlockSpec(dims, lambda *i: (0,) * len(dims))


def struct(*dims, kind=F32):
    return jax.ShapeDtypeStruct(dims, kind)


def estimate(flops, moved):
    return pl.CostEstimate(flops=flops, bytes_accessed=moved, transcendentals=0)


def z_forward_call(volume, table):
    return call(
        z_forward_kernel,
        [struct(2, 4, 16, 2, 8, 128)] * 4,
        (4,),
        [
            pl.BlockSpec((32, 4, 16, Z), lambda i: (0, i, 0, 0)),
            whole(256, 256),
            Placed(256, Z),
        ],
        [pl.BlockSpec((2, 1, 16, 2, 8, 128), lambda i: (0, i, 0, 0, 0, 0))] * 4,
        [pltpu.VMEM((16, 4, 32, Z), BF16)],
        estimate(3 * 2**30, 8 * 2**20),
        60,
        own_place(),
    )(volume, jnp.asarray(swap_table()), table)


def y_forward_call(received, table):
    return call(
        y_forward_kernel,
        struct(16, 16, 2, 8, 128),
        (4,),
        [pl.BlockSpec((1, 1, 256, 128), lambda i: (0, i, 0, 0))] * 4
        + [pl.BlockSpec((4, 1, 256, 128), lambda i: (0, i, 0, 0)), Placed(256, 256)],
        pl.BlockSpec((16, 4, 2, 8, 128), lambda i: (0, i, 0, 0, 0)),
        (),
        estimate(2 * 2**30, 6 * 2**20),
        place=own_place(),
    )(*[block.reshape(block.shape[:-4] + (256, 128)) for block in received], table)


def z_forward_rows_call(volume, table):
    return call(
        z_forward_rows_kernel,
        struct(8, 4, 16, 2, 8, 128),
        (4,),
        [
            pl.BlockSpec((32, 4, 16, Z), lambda i: (0, i, 0, 0)),
            Placed(256, Z),
        ],
        pl.BlockSpec((8, 4, 4, 2, 8, 128), lambda i: (0, 0, i, 0, 0, 0)),
        (),
        estimate(2 * 2**30, 8 * 2**20),
        60,
        own_place(),
    )(volume, table)


def x_forward_rows_call(received):
    return call(
        x_forward_rows_kernel,
        struct(2, 4, 2, 4, 2, 16, 128),
        (4,),
        [
            pl.BlockSpec((8, 1, 256, 128), lambda i: (0, i, 0, 0)),
            whole(128, 256),
        ],
        pl.BlockSpec((2, 1, 2, 4, 2, 16, 128), lambda i: (0, i, 0, 0, 0, 0, 0)),
        (),
        estimate(2**20, 2**16),
    )(received.reshape(8, 4, 256, 128), jnp.asarray(stacked(x_forward())))


def y_forward_rows_call(received, table):
    return call(
        y_forward_rows_kernel,
        struct(2, 2, 4, 128, 128),
        (),
        [whole(4, 128, 128)] * 4 + [Placed(256, 128)],
        whole(2, 2, 4, 128, 128),
        (),
        estimate(2**20, 2**16),
        place=own_place(),
    )(*received, table)


def sum_rows_call(received):
    return call(
        sum_rows_kernel,
        struct(8, 4, 2, 8, 128),
        (),
        [SCALARS] + [whole(4, 128, 128)] * 2,
        whole(8, 4, 2, 8, 128),
        (),
        estimate(2**20, 2**16),
    )(row_place(), *received)


def x_forward_call(received):
    return call(
        x_forward_kernel,
        struct(2, 32, 8, 128),
        (),
        [whole(16, 256, 128), whole(128, 256)],
        whole(2, 32, 8, 128),
        [pltpu.VMEM((4, 256, 128), F32)],
        estimate(2**28, 3 * 2**20),
    )(received.reshape(16, 256, 128), jnp.asarray(stacked(x_forward())))


def mix_call(weight, spectra):
    return call(
        mix_kernel,
        struct(2, 256, 128),
        (4,),
        [
            pl.BlockSpec((2, 32, 64, 128), lambda i: (0, 0, i, 0)),
            whole(2, 32, 8, 128),
        ],
        pl.BlockSpec((2, 64, 128), lambda i: (0, i, 0)),
        (),
        estimate(2**27, 5 * 2**20),
    )(weight, spectra)


def back_call(weight, mixed, partner, target):
    small = whole(2, 256, 128)
    return call(
        back_kernel,
        (struct(2, 32, 8, 128), struct(2, 256, 128)),
        (4,),
        [
            SCALARS,
            pl.BlockSpec((2, 8, 256, 128), lambda i: (0, i, 0, 0)),
            small,
            small,
        ]
        + [whole(2, 4, 2, 8, 128)] * 4
        + [whole(4, 4, 2, 8, 128)],
        (pl.BlockSpec((2, 8, 8, 128), lambda i: (0, i, 0, 0)), small),
        (),
        estimate(2**27, 5 * 2**20),
    )(row_place(), weight, mixed, partner, *target)


def x_inverse_call(back):
    return call(
        x_inverse_kernel,
        [struct(16, 128, 128)] * 2,
        (),
        [whole(2, 32, 8, 128), whole(512, 64)],
        [whole(16, 128, 128)] * 2,
        [pltpu.VMEM((2, 256, 128), F32)],
        estimate(2**28, 3 * 2**20),
    )(back, jnp.asarray(stacked(x_inverse())))


def y_inverse_call(received, table):
    return call(
        y_inverse_kernel,
        [struct(2, 2, 256, 128)] * 4,
        (2,),
        [
            pl.BlockSpec((16, 4, 2, 8, 128), lambda i: (0, i, 0, 0, 0)),
            Placed(512, 128),
        ],
        [pl.BlockSpec((2, 1, 256, 128), lambda i: (0, i, 0, 0))] * 4,
        (),
        estimate(2**30, 3 * 2**20),
        place=own_place(),
    )(received.reshape(16, 8, 2, 8, 128), table)


def z_inverse_call(received, table, half, others):
    return call(
        z_inverse_kernel,
        struct(32, 16, 16, Z, kind=BF16),
        (2,),
        [pl.BlockSpec((1, 1, 16, 2, 8, 128), lambda i: (0, i, 0, 0, 0, 0))] * 4
        + [pl.BlockSpec((4, 1, 16, 2, 8, 128), lambda i: (0, i, 0, 0, 0, 0))]
        + [whole(256, 256), Placed(256, Z)]
        + [pl.BlockSpec(memory_space=pl.ANY)] * len(others),
        pl.BlockSpec((32, 4, 16, Z), lambda i: (0, i + 2 * half, 0, 0)),
        [pltpu.VMEM((16, 4, 32, Z), BF16)],
        estimate(3 * 2**29, 4 * 2**20),
        place=own_place(),
        aliases={8: 0} if others else {},
    )(
        *[block.reshape(block.shape[:-2] + (16, 2, 8, 128)) for block in received],
        jnp.asarray(swap_table()),
        table,
        *others,
    )


def exchange(values, axes):
    return lax.all_to_all(values, axes, split_axis=0, concat_axis=0, tiled=True)


def offset_pairs(offset):
    index = np.arange(math.prod(SHAPE))
    place = np.stack(np.unravel_index(index, SHAPE))
    other = (place + np.array(offset)[:, None]) % np.array(SHAPE)[:, None]
    return list(zip(index.tolist(), np.ravel_multi_index(other, SHAPE).tolist()))


def shifted(values, **steps):
    offset = [steps.get(a, 0) for a in AXES]
    return lax.ppermute(values, AXES, offset_pairs(offset)) if any(offset) else values


def cross(arrived):
    return arrived + [shifted(jnp.stack([block[1] for block in arrived]), core=1)]


def by_place(build):
    return jnp.asarray(
        np.stack([build(y, core, xl) for y in range(4) for core in range(2) for xl in range(2)])
    )


def own_place():
    y, core, xl = (lax.axis_index(a) for a in ("y", "core", "xl"))
    return ((y * 2 + core) * 2 + xl).astype(jnp.int32).reshape(1)


def first_order(y, core, sign):
    return [((y + sign * i) % 4) * 2 + (core + sign * j) % 2 for i in range(4) for j in range(2)]


def z_rows_by_offset(y, core, xl):
    table = z_table().reshape(8, 16, Z)[first_order(y, core, 1)]
    return stacked(table.reshape(128, Z))


def z_rows_by_col(y, core, xl):
    order = [
        (((y + i) % 4) * 2 + (xl + j) % 2) * 2 + (core + k) % 2
        for i in range(4)
        for j in range(2)
        for k in range(2)
    ]
    return stacked(z_table_rows(order))


def y_columns_by_col(y, core, xl):
    return stacked(y_forward_rows([((y - i) % 4 * 2 + xl) * 2 + core for i in range(4)]))


def z_rows_by_source(y, core, xl):
    table = z_table().reshape(8, 16, Z)[first_order(y, core, -1)]
    return stacked(table.reshape(128, Z))


def y_rows_by_offset(y, core, xl):
    table = y_inverse(xl).reshape(8, 32, 128)[first_order(y, core, 1)]
    return stacked(table.reshape(256, 128))


def y_columns_by_offset(y, core, xl):
    table = y_forward(xl).reshape(128, 8, 32)[:, first_order(y, core, -1)]
    return stacked(table.reshape(128, 256))


def plane_pairs():
    index = np.arange(math.prod(SHAPE)).reshape(8, 16)[:, 0].tolist()
    same = [(index[b], index[7 - b]) for b in range(8)]
    edge = [(index[b], index[8 - b]) for b in range(1, 8)]
    return same, edge


def mirrored(mixed):
    same_pairs, edge_pairs = plane_pairs()
    plane = mixed.reshape(2, C, 8, 128)[..., :MX]
    same = lax.ppermute(plane, AXES, same_pairs)
    edge = lax.ppermute(plane[:, :, :1], AXES, edge_pairs)
    by_ky = jnp.concatenate([edge, same[:, :, :0:-1]], 2)
    by_kx = jnp.concatenate([jnp.zeros_like(by_ky[..., :1]), by_ky[..., :0:-1]], 3)
    signed = by_kx * jnp.array([1.0, -1.0], F32)[:, None, None, None]
    padded = jnp.pad(signed, ((0, 0),) * 3 + ((0, 128 - MX),))
    return padded.reshape(2, 256, 128)


def weight_grad(spectra, cotangent):
    real, imag = spectra.reshape(2, 1, C, 1, 8, 4, MX)
    turned = jnp.stack([cotangent[1], -cotangent[0]])
    cotangent, turned = (a.reshape(2, 1, C, 8, 4, MX) for a in (cotangent, turned))
    return (real * cotangent + imag * turned).astype(BF16)


def per_device(voxels, target, weight):
    barrier = lax.optimization_barrier
    packed = weight.reshape(2, C, 256, 128)

    target_lines = z_forward_rows_call(target, by_place(z_rows_by_col))
    target_lines, voxels = barrier((target_lines, voxels))
    target_lines = exchange(target_lines, ROW)
    lines = z_forward_call(voxels, by_place(z_rows_by_offset))
    lines = [shifted(block, y=i) for i, block in enumerate(lines)]
    target_lines, packed = barrier((target_lines, packed))
    blocks = x_forward_rows_call(target_lines).reshape(4, 4, 128, 128)
    lines, blocks = barrier((lines, blocks))
    blocks = [shifted(blocks[i], y=i) for i in range(4)]
    planes = y_forward_call(cross(lines), by_place(y_columns_by_offset))
    planes = exchange(planes, SECOND)
    blocks = y_forward_rows_call(blocks, by_place(y_columns_by_col))
    blocks = blocks[0] + shifted(blocks[1], core=1)
    blocks = [blocks[0], shifted(blocks[1], xl=1)]
    spectra = x_forward_call(planes)
    mixed = mix_call(packed, spectra)
    mixed, blocks = barrier((mixed, blocks))
    mixed, sums = barrier((mixed, sum_rows_call(blocks)))
    arrived = [shifted(sums[2 * i : 2 * i + 2], z=i) for i in range(4)]
    partner = mirrored(mixed)
    partner, arrived = barrier((partner, arrived))
    crossed = shifted(jnp.stack([block[1] for block in arrived]), xh=1)
    back, cotangent = back_call(packed, mixed, partner, arrived + [crossed])
    y_table, z_table_here = by_place(y_rows_by_offset), by_place(z_rows_by_source)
    first, second = x_inverse_call(back)
    first, second = barrier((exchange(first, SECOND), second))
    first = y_inverse_call(first, y_table)
    first = [shifted(block, y=i) for i, block in enumerate(first)]
    second = y_inverse_call(exchange(second, SECOND), y_table)
    first, second = barrier((first, second))
    second = [shifted(block, y=i) for i, block in enumerate(second)]
    grad = weight_grad(spectra, cotangent)
    field = z_inverse_call(cross(first), z_table_here, 0, [])
    second, field, grad = barrier((second, field, grad))
    return z_inverse_call(cross(second), z_table_here, 1, [field]), grad


def solution(mesh):
    fine = Mesh(mesh.devices.reshape(SHAPE), AXES)
    field = P(None, ROW, COL, None)
    modes = P(None, None, None, ROW, COL, None)
    return jax.shard_map(
        per_device,
        mesh=fine,
        in_specs=(field, field, modes),
        out_specs=(field, modes),
        check_vma=False,
    )
```

```python
import functools
import math
import typing

import jax
import jax.numpy as jnp
import ml_dtypes
import numpy as np
from jax import lax
from jax.experimental import pallas as pl
from jax.experimental.pallas import tpu as pltpu
from jax.sharding import Mesh
from jax.sharding import PartitionSpec as P

C = 32
X = 128
Y = 256
Z = 256
MX = 32
MY = 64
MZ = 64

AXES = ("xh", "z", "y", "xl", "core")
SHAPE = (2, 4, 4, 2, 2)
ROW = ("xh", "z")
COL = ("y", "xl", "core")
FIRST = ("y", "core")
SECOND = ("xh", "z", "xl")
F32 = jnp.float32
BF16 = jnp.bfloat16


def split_parts(table):
    high = table.astype(ml_dtypes.bfloat16)
    low = (table - high.astype(np.float64)).astype(ml_dtypes.bfloat16)
    return high, low


def angles(frequency, position, length):
    return 2.0 * np.pi / length * ((frequency[:, None] * position[None, :]) % length)


def kept_z():
    y, core, part, xl, k = np.meshgrid(
        np.arange(4), np.arange(2), np.arange(2), np.arange(2), np.arange(4), indexing="ij"
    )
    return (((y * 2 + xl) * 2 + core) * 4 + k).reshape(-1), part.reshape(-1)


def z_table():
    frequency, part = kept_z()
    angle = angles(frequency, np.arange(Z), Z)
    return np.where(part[:, None] == 0, np.cos(angle), -np.sin(angle)) * Z**-0.5


def rotation(angle, row_part, column_part, sign):
    same = row_part[:, None] == column_part[None, :]
    lower = row_part[:, None] > column_part[None, :]
    return np.where(same, np.cos(angle), np.where(lower, sign, -sign) * np.sin(angle))


def y_points(xl):
    y, core, point, part = np.meshgrid(
        np.arange(4), np.arange(2), np.arange(16), np.arange(2), indexing="ij"
    )
    return (((y * 2 + xl) * 2 + core) * 16 + point).reshape(-1), part.reshape(-1)


def z_table_rows(order):
    half, part, place, k = np.meshgrid(
        np.arange(2), np.arange(2), np.arange(8), np.arange(4), indexing="ij"
    )
    frequency = np.array(order)[half * 8 + place] * 4 + k
    angle = angles(frequency.reshape(-1), np.arange(Z), Z)
    return np.where(part.reshape(-1, 1) == 0, np.cos(angle), -np.sin(angle)) * Z**-0.5


def y_forward_rows(places):
    block, part, point = np.meshgrid(
        np.array(places), np.arange(2), np.arange(16), indexing="ij"
    )
    frequency, row_part = y_modes()
    angle = angles(frequency, (block * 16 + point).reshape(-1), Y)
    return rotation(angle, row_part, part.reshape(-1), -1) * Y**-0.5


def y_modes():
    block, part, j = np.meshgrid(np.arange(8), np.arange(2), np.arange(8), indexing="ij")
    return (block * 8 + j).reshape(-1) - MY // 2, part.reshape(-1)


def y_forward(xl):
    position, column_part = y_points(xl)
    frequency, row_part = y_modes()
    return rotation(angles(frequency, position, Y), row_part, column_part, -1) * Y**-0.5


def y_inverse(xl):
    position, row_part = y_points(xl)
    frequency, column_part = y_modes()
    return rotation(angles(frequency, position, Y).T, row_part, column_part, 1) * Y**-0.5


def x_points():
    return np.repeat(np.arange(X), 2), np.tile(np.arange(2), X)


def x_modes():
    return np.tile(np.arange(MX), 2) - MX // 2, np.repeat(np.arange(2), MX)


def x_forward():
    position, column_part = x_points()
    frequency, row_part = x_modes()
    return rotation(angles(frequency, position, X), row_part, column_part, -1) * X**-0.5


def x_inverse():
    position, row_part = x_points()
    frequency, column_part = x_modes()
    return rotation(angles(frequency, position, X).T, row_part, column_part, 1) * X**-0.5


def stacked(table):
    return np.concatenate(split_parts(table), 0)


def swap_table():
    index = np.arange(256)
    table = np.zeros((256, 256), ml_dtypes.bfloat16)
    table[index, (index % 16) * 16 + index // 16] = 1
    return table


def dot(a, b):
    return jnp.dot(a, b, preferred_element_type=F32)


def halves(values):
    high = values.astype(BF16)
    return high, (values - high.astype(F32)).astype(BF16)


def table_dot(table, values):
    rows = table.shape[0] // 2
    high, low = halves(values)
    both = dot(table, high)
    return both[:rows] + both[rows:] + dot(table[:rows], low)


def swap_quads(tiles):
    lane = lax.broadcasted_iota(jnp.int32, tiles[0].shape, 1) // 32
    result = []
    for b in range(4):
        total = None
        for a in range(4):
            shift = (32 * (a - b)) % 128
            moved = pltpu.roll(tiles[a], shift, 1) if shift else tiles[a]
            total = moved if total is None else jnp.where(lane == a, moved, total)
        result.append(total)
    return result


def by_source(refs):
    crossed = refs[4]
    return [crossed.at[i, 0] if j else refs[i].at[0, 0] for i in range(4) for j in range(2)]


def z_forward_kernel(volume, swap, table, *refs):
    out, rows = refs[:4], refs[4]
    for x in range(4):
        for half in range(2):
            block = volume[half * 16 : half * 16 + 16, x].reshape(256, Z)
            moved = dot(swap[...], block).astype(BF16)
            for y in range(16):
                rows[y, x, half * 16 : half * 16 + 16, :] = moved[y * 16 : y * 16 + 16]
    for pair in range(8):
        points = rows[pair * 2 : pair * 2 + 2].reshape(256, Z)
        both = lax.dot_general(
            table[...], points, (((1,), (1,)), ((), ())), preferred_element_type=F32
        )
        values = both[:128] + both[128:]
        for y in range(2):
            for target in range(8):
                for part in range(2):
                    row = (target * 2 + part) * 8
                    out[target // 2][target % 2, 0, pair * 2 + y, part] = values[
                        row : row + 8, y * 128 : y * 128 + 128
                    ]


def y_forward_kernel(*refs):
    received, table, out = by_source(refs[:5]), refs[5], refs[6]
    for quad in range(2):
        columns = []
        for k in range(4):
            kz = quad * 4 + k
            columns.append(
                jnp.concatenate(
                    [received[s][pl.ds(kz, 32, stride=8), :] for s in range(8)], 0
                )
            )
        values = table_dot(table[...], jnp.concatenate(columns, 1))
        tiles = swap_quads([values[:, k * 128 : k * 128 + 128] for k in range(4)])
        for x in range(4):
            for block in range(8):
                for part in range(2):
                    row = (block * 2 + part) * 8
                    out[block * 2 + quad, x, part] = tiles[x][row : row + 8]


def x_forward_kernel(received, table, out, flat):
    for ky in range(8):
        pieces = []
        for block in range(8):
            first = received[block * 2, pl.ds(ky, 32, stride=8), :]
            second = received[block * 2 + 1, pl.ds(ky, 32, stride=8), :]
            pieces.append(first + second)
        values = table_dot(table[...], jnp.concatenate(pieces, 0))
        for part in range(2):
            flat[2 + part, ky * 32 : ky * 32 + 32] = values[part * 32 : part * 32 + 32]
    for part in range(2):
        for high in range(2):
            turned = flat[2 + part, high * 128 : high * 128 + 128].T
            tiles = swap_quads([turned[k * 32 : k * 32 + 32] for k in range(4)])
            for low in range(4):
                row = (high * 4 + low) * 32
                flat[part, row : row + 32] = tiles[low]
        for c in range(C):
            out[part, c] = flat[part, pl.ds(c, 8, stride=32), :]


def z_forward_rows_kernel(volume, table, out):
    lower = lax.broadcasted_iota(jnp.int32, (64, 128), 1) < 64
    for x in range(4):
        for half in range(2):
            block = volume[half * 16 : half * 16 + 16, x].reshape(256, Z)
            both = lax.dot_general(
                table[...], block, (((1,), (1,)), ((), ())), preferred_element_type=F32
            )
            values = both[:128] + both[128:]
            for pair in range(2):
                tile = values[:, pair * 128 : pair * 128 + 128]
                first, second = tile[:64], tile[64:]
                results = (
                    jnp.where(lower, first, pltpu.roll(second, 64, 1)),
                    jnp.where(lower, pltpu.roll(first, 64, 1), second),
                )
                for e in range(2):
                    target = half * 4 + pair * 2 + e
                    for part in range(2):
                        for group in range(4):
                            row = (part * 4 + group) * 8
                            out[target, group, x, part] = results[e][row : row + 8]


def x_forward_rows_kernel(received, table, out):
    for quad in range(2):
        columns = []
        for k in range(4):
            columns.append(
                jnp.concatenate(
                    [received[s, 0, pl.ds(quad * 4 + k, 32, stride=8), :] for s in range(8)], 0
                )
            )
        values = table_dot(table[...], jnp.concatenate(columns, 1))
        for pair in range(2):
            stack = [values[:, k * 128 : k * 128 + 128] for k in (2 * pair, 2 * pair + 1)]
            turned = jnp.concatenate(stack, 0).T
            for p in range(2):
                rows = [p * 64 + c * 16 for c in range(4)]
                tiles = swap_quads([turned[row : row + 16] for row in rows])
                for k in range(2):
                    for part in range(2):
                        out[p, 0, quad, 2 * pair + k, part] = tiles[2 * k + part]


def y_forward_rows_kernel(*refs):
    received, table, out = refs[:4], refs[4], refs[5]
    for target in range(4):
        columns = []
        for k in range(4):
            rows = slice(k * 32, k * 32 + 32)
            columns.append(jnp.concatenate([received[s][target, rows] for s in range(4)], 0))
        values = table_dot(table[...], jnp.concatenate(columns, 1))
        for k in range(4):
            out[target % 2, target // 2, k] = values[:, k * 128 : k * 128 + 128]


def sum_rows_kernel(place, *refs):
    received, out = refs[:2], refs[2]
    for target in range(8):
        offset = (target % 4 + 4 - place[1]) % 4 * 2 + (target // 4 + 2 - place[0]) % 2
        for k in range(4):
            rows = slice(target * 16, target * 16 + 16)
            total = received[0][k, rows] + received[1][k, rows]
            out[offset, k] = total.reshape(2, 8, 128)


def mix_kernel(weight, spectra, out):
    for o in range(0, 8, 4):
        rows = slice(o * 8, o * 8 + 32)

        def step(c, totals):
            real, imag = totals
            weight_real = weight[0, c, rows].astype(F32)
            weight_imag = weight[1, c, rows].astype(F32)
            field_real = jnp.concatenate([spectra[0, c]] * 4, 0)
            field_imag = jnp.concatenate([spectra[1, c]] * 4, 0)
            real = real + weight_real * field_real - weight_imag * field_imag
            imag = imag + weight_real * field_imag + weight_imag * field_real
            return real, imag

        zero = jnp.zeros((32, 128), F32)
        real, imag = lax.fori_loop(0, C, step, (zero, zero), unroll=4)
        out[0, rows] = real
        out[1, rows] = imag


def back_kernel(*refs):
    place, weight, mixed, partner = refs[:4]
    arrived, crossed, back, cotangent = refs[4:8], refs[8], refs[9], refs[10]
    factor = math.sqrt(X * Y * Z / (MX * MY * MZ))

    @pl.when(pl.program_id(0) == 0)
    def _():
        for part in range(2):
            for offset in range(8):
                i, j = offset // 2, offset % 2
                source = (place[0] + j) % 2 * 4 + (place[1] + 4 - i) % 4
                target = crossed.at[i] if j else arrived[i].at[0]
                tiles = swap_quads([target[k, part] for k in range(4)])
                for c in range(4):
                    rows = pl.ds(pl.multiple_of(source * 32 + c * 8, 8), 8)
                    cotangent[part, rows] = (0.5 * factor * factor) * (
                        mixed[part, rows] + partner[part, rows]
                    ) - factor * tiles[c]

    def step(c, carry):
        real = jnp.zeros((32, 128), F32)
        imag = jnp.zeros((32, 128), F32)
        for o in range(0, C, 4):
            rows = slice(o * 8, o * 8 + 32)
            weight_real = weight[0, c, rows].astype(F32)
            weight_imag = weight[1, c, rows].astype(F32)
            real = real + weight_real * cotangent[0, rows] + weight_imag * cotangent[1, rows]
            imag = imag + weight_real * cotangent[1, rows] - weight_imag * cotangent[0, rows]
        back[0, c] = real[:8] + real[8:16] + real[16:24] + real[24:]
        back[1, c] = imag[:8] + imag[8:16] + imag[16:24] + imag[24:]
        return carry

    lax.fori_loop(0, 8, step, 0)


def x_inverse_kernel(back, table, first, second, flat):
    for part in range(2):
        for c in range(C):
            flat[part, pl.ds(c, 8, stride=32), :] = back[part, c]
    for high in range(2):
        turned = []
        for part in range(2):
            rows = [(high * 4 + low) * 32 for low in range(4)]
            tiles = swap_quads([flat[part, row : row + 32] for row in rows])
            turned.append(jnp.concatenate(tiles, 0).T)
        for low in range(4):
            ky = high * 4 + low
            modes = jnp.concatenate([t[low * 32 : low * 32 + 32] for t in turned], 0)
            values = table_dot(table[...], modes)
            for block in range(8):
                row = block * 32
                for xl in range(2):
                    first[block * 2 + xl, pl.ds(ky, 16, stride=8), :] = values[row : row + 16]
                    second[block * 2 + xl, pl.ds(ky, 16, stride=8), :] = values[
                        row + 16 : row + 32
                    ]


def y_inverse_kernel(received, table, *out):
    for quad in range(2):
        tiles = []
        for x in range(4):
            tiles.append(
                jnp.concatenate(
                    [received[block * 2 + quad, x].reshape(16, 128) for block in range(8)], 0
                )
            )
        columns = swap_quads(tiles)
        values = table_dot(table[...], jnp.concatenate(columns, 1))
        for k in range(4):
            for target in range(8):
                out[target // 2][target % 2, 0, pl.ds(quad * 4 + k, 32, stride=8), :] = values[
                    target * 32 : target * 32 + 32, k * 128 : k * 128 + 128
                ]


def z_inverse_kernel(*refs):
    received, swap, table, out, rows = by_source(refs[:5]), *refs[5:7], *refs[-2:]
    for y in range(16):
        modes = jnp.concatenate([received[s][y].reshape(16, 128) for s in range(8)], 0)
        high, low = halves(modes.T)
        both = jnp.concatenate([high, low], 1)
        first = jnp.concatenate([table[:128], table[:128]], 0)
        values = dot(both, first) + dot(high, table[128:])
        rows[y] = values.astype(BF16).reshape(4, 32, Z)
    for x in range(4):
        for half in range(2):
            block = jnp.concatenate(
                [rows[y, x, half * 16 : half * 16 + 16, :] for y in range(16)], 0
            )
            moved = dot(swap[...], block).astype(BF16)
            out[half * 16 : half * 16 + 16, x] = moved.reshape(16, 16, Z)


SCALARS = pl.BlockSpec(memory_space=pltpu.SMEM)


def row_place():
    return jnp.stack([lax.axis_index("xh"), lax.axis_index("z")]).astype(jnp.int32)


def call(
    kernel, out, grid, in_specs, out_specs, scratch=(), cost=None, grant=40, place=None, aliases={}
):
    params = pltpu.CompilerParams(vmem_limit_bytes=grant * 2**20)
    if place is None:
        return pl.pallas_call(
            kernel,
            out_shape=out,
            grid=grid,
            in_specs=in_specs,
            out_specs=out_specs,
            scratch_shapes=list(scratch),
            compiler_params=params,
            cost_estimate=cost,
        )

    def fit(spec):
        if isinstance(spec, Placed):
            return pl.BlockSpec((None, spec.rows, spec.columns), lambda *a: (a[-1][0], 0, 0))
        if spec.index_map is None:
            return spec
        return pl.BlockSpec(spec.block_shape, lambda *a: spec.index_map(*a[:-1]))

    specs = [fit(spec) for spec in in_specs]
    single = isinstance(out_specs, pl.BlockSpec)
    built = pl.pallas_call(
        lambda index, *refs: kernel(*refs),
        out_shape=out,
        grid_spec=pltpu.PrefetchScalarGridSpec(
            num_scalar_prefetch=1,
            grid=grid or (1,),
            in_specs=specs,
            out_specs=fit(out_specs) if single else [fit(spec) for spec in out_specs],
            scratch_shapes=list(scratch),
        ),
        input_output_aliases=aliases,
        compiler_params=params,
        cost_estimate=cost,
    )
    return lambda *operands: built(place, *operands)


class Placed(typing.NamedTuple):
    rows: int
    columns: int


def whole(*dims):
    return pl.BlockSpec(dims, lambda *i: (0,) * len(dims))


def struct(*dims, kind=F32):
    return jax.ShapeDtypeStruct(dims, kind)


def estimate(flops, moved):
    return pl.CostEstimate(flops=flops, bytes_accessed=moved, transcendentals=0)


def z_forward_call(volume, table):
    return call(
        z_forward_kernel,
        [struct(2, 4, 16, 2, 8, 128)] * 4,
        (4,),
        [
            pl.BlockSpec((32, 4, 16, Z), lambda i: (0, i, 0, 0)),
            whole(256, 256),
            Placed(256, Z),
        ],
        [pl.BlockSpec((2, 1, 16, 2, 8, 128), lambda i: (0, i, 0, 0, 0, 0))] * 4,
        [pltpu.VMEM((16, 4, 32, Z), BF16)],
        estimate(3 * 2**30, 8 * 2**20),
        60,
        own_place(),
    )(volume, jnp.asarray(swap_table()), table)


def y_forward_call(received, table):
    return call(
        y_forward_kernel,
        struct(16, 16, 2, 8, 128),
        (4,),
        [pl.BlockSpec((1, 1, 256, 128), lambda i: (0, i, 0, 0))] * 4
        + [pl.BlockSpec((4, 1, 256, 128), lambda i: (0, i, 0, 0)), Placed(256, 256)],
        pl.BlockSpec((16, 4, 2, 8, 128), lambda i: (0, i, 0, 0, 0)),
        (),
        estimate(2 * 2**30, 6 * 2**20),
        place=own_place(),
    )(*[block.reshape(block.shape[:-4] + (256, 128)) for block in received], table)


def z_forward_rows_call(volume, table):
    return call(
        z_forward_rows_kernel,
        struct(8, 4, 16, 2, 8, 128),
        (4,),
        [
            pl.BlockSpec((32, 4, 16, Z), lambda i: (0, i, 0, 0)),
            Placed(256, Z),
        ],
        pl.BlockSpec((8, 4, 4, 2, 8, 128), lambda i: (0, 0, i, 0, 0, 0)),
        (),
        estimate(2 * 2**30, 8 * 2**20),
        60,
        own_place(),
    )(volume, table)


def x_forward_rows_call(received):
    return call(
        x_forward_rows_kernel,
        struct(2, 4, 2, 4, 2, 16, 128),
        (4,),
        [
            pl.BlockSpec((8, 1, 256, 128), lambda i: (0, i, 0, 0)),
            whole(128, 256),
        ],
        pl.BlockSpec((2, 1, 2, 4, 2, 16, 128), lambda i: (0, i, 0, 0, 0, 0, 0)),
        (),
        estimate(2**20, 2**16),
    )(received.reshape(8, 4, 256, 128), jnp.asarray(stacked(x_forward())))


def y_forward_rows_call(received, table):
    return call(
        y_forward_rows_kernel,
        struct(2, 2, 4, 128, 128),
        (),
        [whole(4, 128, 128)] * 4 + [Placed(256, 128)],
        whole(2, 2, 4, 128, 128),
        (),
        estimate(2**20, 2**16),
        place=own_place(),
    )(*received, table)


def sum_rows_call(received):
    return call(
        sum_rows_kernel,
        struct(8, 4, 2, 8, 128),
        (),
        [SCALARS] + [whole(4, 128, 128)] * 2,
        whole(8, 4, 2, 8, 128),
        (),
        estimate(2**20, 2**16),
    )(row_place(), *received)


def x_forward_call(received):
    return call(
        x_forward_kernel,
        struct(2, 32, 8, 128),
        (),
        [whole(16, 256, 128), whole(128, 256)],
        whole(2, 32, 8, 128),
        [pltpu.VMEM((4, 256, 128), F32)],
        estimate(2**28, 3 * 2**20),
    )(received.reshape(16, 256, 128), jnp.asarray(stacked(x_forward())))


def mix_call(weight, spectra):
    return call(
        mix_kernel,
        struct(2, 256, 128),
        (4,),
        [
            pl.BlockSpec((2, 32, 64, 128), lambda i: (0, 0, i, 0)),
            whole(2, 32, 8, 128),
        ],
        pl.BlockSpec((2, 64, 128), lambda i: (0, i, 0)),
        (),
        estimate(2**27, 5 * 2**20),
    )(weight, spectra)


def back_call(weight, mixed, partner, target):
    small = whole(2, 256, 128)
    return call(
        back_kernel,
        (struct(2, 32, 8, 128), struct(2, 256, 128)),
        (4,),
        [
            SCALARS,
            pl.BlockSpec((2, 8, 256, 128), lambda i: (0, i, 0, 0)),
            small,
            small,
        ]
        + [whole(2, 4, 2, 8, 128)] * 4
        + [whole(4, 4, 2, 8, 128)],
        (pl.BlockSpec((2, 8, 8, 128), lambda i: (0, i, 0, 0)), small),
        (),
        estimate(2**27, 5 * 2**20),
    )(row_place(), weight, mixed, partner, *target)


def x_inverse_call(back):
    return call(
        x_inverse_kernel,
        [struct(16, 128, 128)] * 2,
        (),
        [whole(2, 32, 8, 128), whole(512, 64)],
        [whole(16, 128, 128)] * 2,
        [pltpu.VMEM((2, 256, 128), F32)],
        estimate(2**28, 3 * 2**20),
    )(back, jnp.asarray(stacked(x_inverse())))


def y_inverse_call(received, table):
    return call(
        y_inverse_kernel,
        [struct(2, 2, 256, 128)] * 4,
        (2,),
        [
            pl.BlockSpec((16, 4, 2, 8, 128), lambda i: (0, i, 0, 0, 0)),
            Placed(512, 128),
        ],
        [pl.BlockSpec((2, 1, 256, 128), lambda i: (0, i, 0, 0))] * 4,
        (),
        estimate(2**30, 3 * 2**20),
        place=own_place(),
    )(received.reshape(16, 8, 2, 8, 128), table)


def z_inverse_call(received, table, half, others):
    return call(
        z_inverse_kernel,
        struct(32, 16, 16, Z, kind=BF16),
        (2,),
        [pl.BlockSpec((1, 1, 16, 2, 8, 128), lambda i: (0, i, 0, 0, 0, 0))] * 4
        + [pl.BlockSpec((4, 1, 16, 2, 8, 128), lambda i: (0, i, 0, 0, 0, 0))]
        + [whole(256, 256), Placed(256, Z)]
        + [pl.BlockSpec(memory_space=pl.ANY)] * len(others),
        pl.BlockSpec((32, 4, 16, Z), lambda i: (0, i + 2 * half, 0, 0)),
        [pltpu.VMEM((16, 4, 32, Z), BF16)],
        estimate(3 * 2**29, 4 * 2**20),
        place=own_place(),
        aliases={8: 0} if others else {},
    )(
        *[block.reshape(block.shape[:-2] + (16, 2, 8, 128)) for block in received],
        jnp.asarray(swap_table()),
        table,
        *others,
    )


def exchange(values, axes):
    return lax.all_to_all(values, axes, split_axis=0, concat_axis=0, tiled=True)


def offset_pairs(offset):
    index = np.arange(math.prod(SHAPE))
    place = np.stack(np.unravel_index(index, SHAPE))
    other = (place + np.array(offset)[:, None]) % np.array(SHAPE)[:, None]
    return list(zip(index.tolist(), np.ravel_multi_index(other, SHAPE).tolist()))


def shifted(values, **steps):
    offset = [steps.get(a, 0) for a in AXES]
    return lax.ppermute(values, AXES, offset_pairs(offset)) if any(offset) else values


def cross(arrived):
    return arrived + [shifted(jnp.stack([block[1] for block in arrived]), core=1)]


def by_place(build):
    return jnp.asarray(
        np.stack([build(y, core, xl) for y in range(4) for core in range(2) for xl in range(2)])
    )


def own_place():
    y, core, xl = (lax.axis_index(a) for a in ("y", "core", "xl"))
    return ((y * 2 + core) * 2 + xl).astype(jnp.int32).reshape(1)


def first_order(y, core, sign):
    return [((y + sign * i) % 4) * 2 + (core + sign * j) % 2 for i in range(4) for j in range(2)]


def z_rows_by_offset(y, core, xl):
    table = z_table().reshape(8, 16, Z)[first_order(y, core, 1)]
    return stacked(table.reshape(128, Z))


def z_rows_by_col(y, core, xl):
    order = [
        (((y + i) % 4) * 2 + (xl + j) % 2) * 2 + (core + k) % 2
        for i in range(4)
        for j in range(2)
        for k in range(2)
    ]
    return stacked(z_table_rows(order))


def y_columns_by_col(y, core, xl):
    return stacked(y_forward_rows([((y - i) % 4 * 2 + xl) * 2 + core for i in range(4)]))


def z_rows_by_source(y, core, xl):
    table = z_table().reshape(8, 16, Z)[first_order(y, core, -1)]
    return stacked(table.reshape(128, Z))


def y_rows_by_offset(y, core, xl):
    table = y_inverse(xl).reshape(8, 32, 128)[first_order(y, core, 1)]
    return stacked(table.reshape(256, 128))


def y_columns_by_offset(y, core, xl):
    table = y_forward(xl).reshape(128, 8, 32)[:, first_order(y, core, -1)]
    return stacked(table.reshape(128, 256))


def plane_pairs():
    index = np.arange(math.prod(SHAPE)).reshape(8, 16)[:, 0].tolist()
    same = [(index[b], index[7 - b]) for b in range(8)]
    edge = [(index[b], index[8 - b]) for b in range(1, 8)]
    return same, edge


def mirrored(mixed):
    same_pairs, edge_pairs = plane_pairs()
    plane = mixed.reshape(2, C, 8, 128)[..., :MX]
    same = lax.ppermute(plane, AXES, same_pairs)
    edge = lax.ppermute(plane[:, :, :1], AXES, edge_pairs)
    by_ky = jnp.concatenate([edge, same[:, :, :0:-1]], 2)
    by_kx = jnp.concatenate([jnp.zeros_like(by_ky[..., :1]), by_ky[..., :0:-1]], 3)
    signed = by_kx * jnp.array([1.0, -1.0], F32)[:, None, None, None]
    padded = jnp.pad(signed, ((0, 0),) * 3 + ((0, 128 - MX),))
    return padded.reshape(2, 256, 128)


def weight_grad(spectra, cotangent):
    real, imag = spectra.reshape(2, 1, C, 1, 8, 4, MX)
    turned = jnp.stack([cotangent[1], -cotangent[0]])
    cotangent, turned = (a.reshape(2, 1, C, 8, 4, MX) for a in (cotangent, turned))
    return (real * cotangent + imag * turned).astype(BF16)


def per_device(voxels, target, weight):
    barrier = lax.optimization_barrier
    packed = weight.reshape(2, C, 256, 128)

    target_lines = z_forward_rows_call(target, by_place(z_rows_by_col))
    target_lines, voxels = barrier((target_lines, voxels))
    target_lines = exchange(target_lines, ROW)
    lines = z_forward_call(voxels, by_place(z_rows_by_offset))
    lines = [shifted(block, y=i) for i, block in enumerate(lines)]
    target_lines, packed = barrier((target_lines, packed))
    blocks = x_forward_rows_call(target_lines).reshape(4, 4, 128, 128)
    lines, blocks = barrier((lines, blocks))
    blocks = [shifted(blocks[i], y=i) for i in range(4)]
    planes = y_forward_call(cross(lines), by_place(y_columns_by_offset))
    planes = exchange(planes, SECOND)
    blocks = y_forward_rows_call(blocks, by_place(y_columns_by_col))
    blocks = blocks[0] + shifted(blocks[1], core=1)
    blocks = [blocks[0], shifted(blocks[1], xl=1)]
    spectra = x_forward_call(planes)
    mixed = mix_call(packed, spectra)
    mixed, blocks = barrier((mixed, blocks))
    sums = sum_rows_call(blocks)
    arrived = [shifted(sums[2 * i : 2 * i + 2], z=i) for i in range(4)]
    mixed, arrived = barrier((mixed, arrived))
    partner = mirrored(mixed)
    crossed = shifted(jnp.stack([block[1] for block in arrived]), xh=1)
    back, cotangent = back_call(packed, mixed, partner, arrived + [crossed])
    y_table, z_table_here = by_place(y_rows_by_offset), by_place(z_rows_by_source)
    first, second = x_inverse_call(back)
    first, second = barrier((exchange(first, SECOND), second))
    first = y_inverse_call(first, y_table)
    first = [shifted(block, y=i) for i, block in enumerate(first)]
    second = y_inverse_call(exchange(second, SECOND), y_table)
    first, second = barrier((first, second))
    second = [shifted(block, y=i) for i, block in enumerate(second)]
    grad = weight_grad(spectra, cotangent)
    field = z_inverse_call(cross(first), z_table_here, 0, [])
    second, field, grad = barrier((second, field, grad))
    return z_inverse_call(cross(second), z_table_here, 1, [field]), grad


def solution(mesh):
    fine = Mesh(mesh.devices.reshape(SHAPE), AXES)
    field = P(None, ROW, COL, None)
    modes = P(None, None, None, ROW, COL, None)
    return jax.shard_map(
        per_device,
        mesh=fine,
        in_specs=(field, field, modes),
        out_specs=(field, modes),
        check_vma=False,
    )
```
